32 devices in a mesh: seq: 8 (over z, x), head: 4 (over y, core).
Axes of the slice: x: 2, y: 2, z: 4, core: 2. Of those that a mesh axis runs over, the one named last changes fastest.
Arguments:
- queries: bfloat16 [8192, 4096], P(('seq', 'head')), may hold values from -5 to 5
- keys: bfloat16 [8192, 1024], P(('seq', 'head')), may hold values from -5 to 5
- values: bfloat16 [8192, 1024], P(('seq', 'head')), may hold values from -6 to 6
- upstream: bfloat16 [8192, 4096], P('seq', 'head'), may hold values from -6 to 6
- lengths: int32 [8, 8], P('seq'), may hold values from 1 to 122, as said below
- guests: int32 [8, 8], P('seq'), may hold values from 0 to 1, as said below
- advantage: float32 [8, 8], P('seq'), may hold values from -4 to 4
- partner: int32 [8], replicated, may hold values from 0 to 7, as said below
Outputs:
- grad_q: bfloat16 [8192, 4096], P(('seq', 'head'))
- grad_k: bfloat16 [8192, 1024], P(('seq', 'head'))
- grad_v: bfloat16 [8192, 1024], P(('seq', 'head'))
The draws below stay inside these ranges and needn't reach their ends.
Inputs may be any that keep to these rules, and one draw needn't show every extreme that they name: `lengths`: every tree has a slot with a response of 122 tokens; rows of a slot beyond its length are padding. `guests`: every tree has at least one guest slot. The pairing is mutual and never pairs a tree with itself: partner[partner[i]] = i.
All inputs are finite; a program needn't handle non-finite values.
Results may differ from the reference program's by a relative error of at most 0.025.
Values may be sent and summed in bfloat16 or wider, within the bound.
A program may use at most 64 MiB of HBM per device.

```python
import jax
import jax.numpy as jnp
from jax import lax

KV_HEADS = 8
HEAD_DIM = 128
D = 4096
PROMPT = 48
RESP = 8
RESP_LEN = 122
GROUP = 4
KV_WIDTH = 1024
ROWS = 1024
TREES = 8


def draw_queries(key, part):
    own_key = jax.random.fold_in(key, 1)
    array_shape = (TREES, ROWS, KV_HEADS, GROUP, HEAD_DIM)
    values_out = jnp.clip(jax.random.normal(own_key, array_shape), -5.0, 5.0)
    return values_out.reshape(TREES * ROWS, D).astype(jnp.bfloat16)


def draw_keys(key, part):
    own_key = jax.random.fold_in(key, 2)
    array_shape = (TREES, ROWS, KV_HEADS, HEAD_DIM)
    values_out = jnp.clip(jax.random.normal(own_key, array_shape), -5.0, 5.0)
    return values_out.reshape(TREES * ROWS, KV_WIDTH).astype(jnp.bfloat16)


def draw_lengths(key, part):
    first_key = jax.random.fold_in(key, 3)
    second_key = jax.random.fold_in(key, 4)
    drawn = jax.random.randint(first_key, (TREES, RESP), 1, RESP_LEN + 1)
    longest = jax.random.randint(second_key, (TREES,), 0, RESP)
    slot_index = jnp.arange(RESP)[None, :]
    return jnp.where(slot_index == longest[:, None], RESP_LEN, drawn).astype(jnp.int32)


def draw_guests(key, part):
    coins = jax.random.randint(jax.random.fold_in(key, 6), (TREES, RESP), 0, 2)
    forced = jax.random.randint(jax.random.fold_in(key, 7), (TREES,), 0, RESP)
    slot_index = jnp.arange(RESP)[None, :]
    return jnp.where(slot_index == forced[:, None], 1, coins).astype(jnp.int32)


def draw_partner(key, part):
    halfway = TREES // 2
    first_tree = jax.random.randint(jax.random.fold_in(key, 8), (), 0, halfway)
    second_tree = first_tree + halfway
    order = jax.random.permutation(jax.random.fold_in(key, 5), TREES).astype(jnp.int32)
    rank = jnp.zeros((TREES,), jnp.int32).at[order].set(jnp.arange(TREES, dtype=jnp.int32))
    index = jnp.arange(TREES, dtype=jnp.int32)
    scores = jnp.where(index == first_tree, -2, jnp.where(index == second_tree, -1, rank))
    arranged = jnp.argsort(scores, stable=True).astype(jnp.int32)
    left_trees = arranged[0::2]
    right_trees = arranged[1::2]
    paired = jnp.zeros((TREES,), jnp.int32)
    paired = paired.at[left_trees].set(right_trees)
    paired = paired.at[right_trees].set(left_trees)
    return paired


def level_of(rng, dims, cuts, low, top_value):
    gain = 1.0
    for position, parts in cuts:
        steps = jax.random.uniform(jax.random.fold_in(jax.random.fold_in(rng, 6), position), (parts,), jnp.float32, low / len(cuts), top_value / len(cuts))
        gain = gain * jnp.repeat(jnp.exp(steps), dims[position] // parts).reshape((-1,) + (1,) * (len(dims) - 1 - position))
    return gain


def gaussian(key, dims, width, bound, split=(), kind=jnp.bfloat16):
    entries = jax.random.normal(key, dims, jnp.float32) * width
    if len(split) > 0:
        entries = level_of(key, dims, split, -0.22, 0.18) * entries
    return jnp.clip(entries, min=-bound, max=bound).astype(kind)


def setup_inputs(seed: int = 0) -> dict:
    streams_of = jax.random.split(jax.random.key(seed), 9)
    return {
        "queries": draw_queries(jax.random.fold_in(streams_of[8], 71), 0),
        "keys": draw_keys(jax.random.fold_in(streams_of[8], 71), 0),
        "values": gaussian(streams_of[2], (TREES * ROWS, KV_WIDTH), 1.0, 6.0, ((0, 32),)),
        "upstream": gaussian(streams_of[3], (TREES * ROWS, D), 1.0, 6.0, ((0, 8), (1, 4))),
        "lengths": draw_lengths(jax.random.fold_in(streams_of[8], 71), 0),
        "guests": draw_guests(jax.random.fold_in(streams_of[8], 71), 0),
        "advantage": gaussian(streams_of[6], (TREES, RESP), 1.0, 4.0, ((0, 8),), jnp.float32),
        "partner": draw_partner(jax.random.fold_in(streams_of[8], 71), 0),
    }


def product(form, left, right):
    return jnp.einsum(form, left.astype(jnp.float32), right.astype(jnp.float32))


def forward_block(q_blk, key_blk, val_blk, allowed):
    scaling = q_blk.shape[-1] ** -0.5
    scores = product('blhgd,bkhd->bhglk', q_blk, key_blk) * scaling
    scores = jnp.where(allowed, scores, -jnp.inf)
    highest = jnp.max(scores, axis=-1, keepdims=True)
    lifted = jnp.exp(scores - highest)
    prob_full = lifted / jnp.sum(lifted, axis=-1, keepdims=True)
    prob_low = lax.optimization_barrier(prob_full.astype(jnp.bfloat16))
    output = product('bhglk,bkhd->blhgd', prob_low, val_blk)
    return prob_full, prob_low, output


def backward_block(prob_full, prob_low, output, q_blk, key_blk, val_blk, cot_blk):
    scaling = q_blk.shape[-1] ** -0.5
    grad_val = product('bhglk,blhgd->bkhd', prob_low, cot_blk)
    grad_prob = product('blhgd,bkhd->bhglk', cot_blk, val_blk)
    row_inner = jnp.sum(cot_blk.astype(jnp.float32) * output, axis=-1)
    row_inner = jnp.transpose(row_inner, (0, 2, 3, 1))[..., None]
    grad_score = prob_full * (grad_prob - row_inner) * scaling
    score_low = lax.optimization_barrier(grad_score.astype(jnp.bfloat16))
    grad_query = product('bhglk,bkhd->blhgd', score_low, key_blk)
    grad_key = product('bhglk,blhgd->bkhd', score_low, q_blk)
    return grad_query, grad_key, grad_val


def tree_pass(q_tree, k_tree, v_tree, far_keys, far_vals, cot_tree, lens_tree, guest_tree, adv_tree):
    heads_kv = k_tree.shape[1]
    group_size = q_tree.shape[2]
    head_width = q_tree.shape[3]
    slot_rows = jnp.arange(RESP_LEN, dtype=jnp.int32)
    valid_slot = (slot_rows[None, :] < lens_tree[:, None]).astype(jnp.float32)
    weighting = valid_slot * adv_tree[:, None]
    cot_slot = cot_tree[PROMPT:].astype(jnp.float32).reshape(RESP, RESP_LEN, heads_kv, group_size, head_width)
    cot_slot = lax.optimization_barrier((cot_slot * weighting[:, :, None, None, None]).astype(jnp.bfloat16))
    q_prompt = q_tree[:PROMPT][None]
    k_prompt = k_tree[:PROMPT][None]
    v_prompt = v_tree[:PROMPT][None]
    prompt_rows = jnp.arange(PROMPT, dtype=jnp.int32)
    causal = prompt_rows[:, None] >= prompt_rows[None, :]
    prob_full, prob_low, out_prompt = forward_block(q_prompt, k_prompt, v_prompt, causal)
    dq_prompt, dk_prompt, dv_prompt = backward_block(prob_full, prob_low, out_prompt, q_prompt, k_prompt, v_prompt, cot_tree[:PROMPT][None])
    chosen = (guest_tree == 1)[:, None, None, None]
    pre_keys = jnp.where(chosen, far_keys[None], k_tree[:PROMPT][None])
    pre_vals = jnp.where(chosen, far_vals[None], v_tree[:PROMPT][None])
    keys_slot = jnp.concatenate([pre_keys, k_tree[PROMPT:].reshape(RESP, RESP_LEN, heads_kv, head_width)], axis=1)
    vals_slot = jnp.concatenate([pre_vals, v_tree[PROMPT:].reshape(RESP, RESP_LEN, heads_kv, head_width)], axis=1)
    columns = jnp.arange(PROMPT + RESP_LEN, dtype=jnp.int32)
    allowed = (columns[None, :] < PROMPT) | (columns[None, :] - PROMPT <= slot_rows[:, None])
    q_slot = q_tree[PROMPT:].reshape(RESP, RESP_LEN, heads_kv, group_size, head_width)
    prob_full, prob_low, out_slot = forward_block(q_slot, keys_slot, vals_slot, allowed)
    out_slot = out_slot * valid_slot[:, :, None, None, None]
    dq_slot, dk_slot, dv_slot = backward_block(prob_full, prob_low, out_slot, q_slot, keys_slot, vals_slot, cot_slot)
    guest_f = guest_tree.astype(jnp.float32)[:, None, None, None]
    own_dk = dk_prompt[0] + jnp.sum((1.0 - guest_f) * dk_slot[:, :PROMPT], axis=0)
    own_dv = dv_prompt[0] + jnp.sum((1.0 - guest_f) * dv_slot[:, :PROMPT], axis=0)
    far_dk = jnp.sum(guest_f * dk_slot[:, :PROMPT], axis=0)
    far_dv = jnp.sum(guest_f * dv_slot[:, :PROMPT], axis=0)
    grad_k = jnp.concatenate([own_dk, dk_slot[:, PROMPT:].reshape(RESP * RESP_LEN, heads_kv, head_width)], axis=0)
    grad_v = jnp.concatenate([own_dv, dv_slot[:, PROMPT:].reshape(RESP * RESP_LEN, heads_kv, head_width)], axis=0)
    grad_q = jnp.concatenate([dq_prompt[0], dq_slot.reshape(RESP * RESP_LEN, heads_kv, group_size, head_width)], axis=0)
    return grad_q, grad_k, grad_v, far_dk, far_dv


def reference(queries, keys, values, upstream, lengths, guests, advantage, partner):
    q_all = queries.reshape(TREES, ROWS, KV_HEADS, GROUP, HEAD_DIM)
    k_all = keys.reshape(TREES, ROWS, KV_HEADS, HEAD_DIM)
    v_all = values.reshape(TREES, ROWS, KV_HEADS, HEAD_DIM)
    cot_all = upstream.reshape(TREES, ROWS, KV_HEADS, GROUP, HEAD_DIM)
    far_keys = k_all[partner, :PROMPT]
    far_vals = v_all[partner, :PROMPT]

    def one_tree(items):
        return tree_pass(*items)

    grad_q, grad_k, grad_v, far_dk, far_dv = lax.map(one_tree, (q_all, k_all, v_all, far_keys, far_vals, cot_all, lengths, guests, advantage))
    grad_k = grad_k.at[:, :PROMPT].add(far_dk[partner])
    grad_v = grad_v.at[:, :PROMPT].add(far_dv[partner])
    return (grad_q.astype(jnp.bfloat16).reshape(TREES * ROWS, D), grad_k.astype(jnp.bfloat16).reshape(TREES * ROWS, KV_WIDTH), grad_v.astype(jnp.bfloat16).reshape(TREES * ROWS, KV_WIDTH))
```

```python
import functools
import math

import jax
import jax.numpy as jnp
from jax import lax
from jax.experimental import pallas as pl
from jax.experimental.pallas import tpu as pltpu
from jax.sharding import PartitionSpec as P

HEAD_DIM = 128
PROMPT = 48
RESP_LEN = 122
TILE = 128
PAD = 128
HALO = 128
LOGICAL = pl.DeviceIdType.MESH
BF16 = jnp.bfloat16
F32 = jnp.float32


def mix(a, b, size):
    out = 0
    bit = 1
    while bit < size:
        out = out + lax.rem(lax.div(a, bit) + lax.div(b, bit), 2) * bit
        bit *= 2
    return out


def dot(a, b, da, db):
    return lax.dot_general(a, b, (((da,), (db,)), ((), ())), preferred_element_type=F32)


def kernel(
    heads, trees, kv_heads, group, resp,
    len_ref, guest_ref, adv_ref, partner_ref,
    q_hbm, k_hbm, v_hbm, up_hbm,
    gq_hbm, gk_hbm, gv_hbm,
    qv, cot, kx, vx, bias, weight, held, far, gqv, pg, pf, rg, hg, hr, acc, back, fin, fout, gkv, gvv,
    loc, cloc, csend, crecv, hsend, hrecv, psend, precv, gsend, grecv, fsend, frecv,
    pgsend, pgrecv, hgsend, hgrecv, bsend, brecv, finsend, finrecv, oq, okv,
):
    h = lax.axis_index("head")
    s = lax.axis_index("seq")
    rows = q_hbm.shape[0]
    tiles = rows // TILE
    local_kv = kv_heads // heads
    width = group * HEAD_DIM
    kw = local_kv * HEAD_DIM
    scaling = HEAD_DIM ** (-0.5)

    def send(src, dst, ssem, rsem, **where):
        return pltpu.make_async_remote_copy(
            src_ref=src, dst_ref=dst, send_sem=ssem, recv_sem=rsem, device_id=where, device_id_type=LOGICAL
        )

    def local(src, dst, sem):
        return pltpu.make_async_copy(src, dst, sem)

    own_copies = [
        local(k_hbm, kx.at[pl.ds(PAD + HALO, rows)], loc.at[0]),
        local(v_hbm, vx.at[pl.ds(PAD + HALO, rows)], loc.at[1]),
        local(q_hbm, qv, loc.at[2]),
    ]
    own_prompt = [
        local(k_hbm.at[pl.ds(0, PROMPT)], kx.at[pl.ds(0, PROMPT)], loc.at[3]),
        local(v_hbm.at[pl.ds(0, PROMPT)], vx.at[pl.ds(0, PROMPT)], loc.at[4]),
    ]
    own_cot = [
        local(
            up_hbm.at[pl.ds(pl.multiple_of(h * rows, TILE), rows), pl.ds(i * width, width)],
            cot.at[h * local_kv + i],
            cloc.at[i],
        )
        for i in range(local_kv)
    ]

    barrier = pltpu.get_barrier_semaphore()
    for m in range(1, heads):
        pl.semaphore_signal(barrier, inc=1, device_id={"head": mix(h, m, heads)}, device_id_type=LOGICAL)

    @pl.loop(1, trees)
    def _(d):
        pl.semaphore_signal(barrier, inc=1, device_id={"seq": lax.rem(s + d, trees)}, device_id_type=LOGICAL)

    @pl.when(h == 0)
    def _():
        for c in own_prompt:
            c.start()

    for c in own_copies + own_cot:
        c.start()
    pl.semaphore_wait(barrier, heads + trees - 2)

    def prompt_copy(a, to):
        src, dst = ((k_hbm, kx), (v_hbm, vx))[a]
        return send(
            src.at[pl.ds(0, PROMPT)], dst.at[pl.ds(0, PROMPT)], psend.at[a, to], precv.at[a], head=to
        )

    def halo_copy(a, to):
        src, dst = ((k_hbm, kx), (v_hbm, vx))[a]
        return send(
            src.at[pl.ds(rows - HALO, HALO)], dst.at[pl.ds(PAD, HALO)], hsend.at[a], hrecv.at[a], head=to
        )

    def cot_copy(m, i):
        p = mix(h, m, heads)
        return send(
            up_hbm.at[pl.ds(pl.multiple_of(p * rows, TILE), rows), pl.ds(i * width, width)],
            cot.at[h * local_kv + i],
            csend.at[m * local_kv + i],
            crecv.at[h * local_kv + i],
            head=p,
        )

    @pl.when(h == 0)
    def _():
        for to in range(1, heads):
            for a in range(2):
                prompt_copy(a, to).start()

    @pl.when(h < heads - 1)
    def _():
        for a in range(2):
            halo_copy(a, h + 1).start()

    order = [m for m in range(2, heads)] + [1]
    for m in order:
        for i in range(local_kv):
            cot_copy(m, i).start()

    zero_pad = jnp.zeros((PAD - 2 * PROMPT, kx.shape[1]), BF16)
    kx[pl.ds(2 * PROMPT, PAD - 2 * PROMPT), :] = zero_pad
    vx[pl.ds(2 * PROMPT, PAD - 2 * PROMPT), :] = zero_pad

    @pl.when(h == 0)
    def _():
        zero_halo = jnp.zeros((HALO, kx.shape[1]), BF16)
        kx[pl.ds(PAD, HALO), :] = zero_halo
        vx[pl.ds(PAD, HALO), :] = zero_halo
        for c in own_prompt:
            c.wait()

    @pl.when(h > 0)
    def _():
        for a in range(2):
            prompt_copy(a, h).wait_recv()

    mine = pl.multiple_of(h * kw, HEAD_DIM)
    held[s, :, 0:kw] = kx[0:PROMPT, pl.ds(mine, kw)]
    held[s, :, kw : 2 * kw] = vx[0:PROMPT, pl.ds(mine, kw)]

    def held_copy(slot, to):
        return send(held.at[slot], held.at[slot], gsend.at[to], grecv.at[slot], seq=to)

    @pl.loop(1, trees)
    def _(d):
        held_copy(s, lax.rem(s + d, trees)).start()

    row_w = lax.broadcasted_iota(jnp.int32, (rows, HEAD_DIM), 0) + h * rows
    w = jnp.ones((rows, HEAD_DIM), F32)
    for r in range(resp):
        begin = PROMPT + r * RESP_LEN
        inside = (row_w >= begin) & (row_w < begin + RESP_LEN)
        w = jnp.where(inside, jnp.where(row_w - begin < len_ref[0, r], adv_ref[0, r], 0.0), w)
    weight[...] = w
    for t in range(tiles):
        row = lax.broadcasted_iota(jnp.int32, (8, TILE), 1) + (h * rows + t * TILE)
        begin_of = jnp.full((8, TILE), 1 << 20, jnp.int32)
        guest = jnp.zeros((8, TILE), jnp.int32)
        for r in range(resp):
            begin = PROMPT + r * RESP_LEN
            inside = (row >= begin) & (row < begin + RESP_LEN)
            begin_of = jnp.where(inside, begin, begin_of)
            guest = jnp.where(inside, guest_ref[0, r], guest)
        row, begin_of, guest = row[0:1], begin_of[0:1], guest[0:1]
        col = lax.broadcasted_iota(jnp.int32, (PAD, TILE), 0)
        seen_own = (col < PROMPT) & (guest == 0) & (col <= row)
        seen_far = (col >= PROMPT) & (col < 2 * PROMPT) & (guest == 1)
        bias[t, 0:PAD, :] = jnp.where(seen_own | seen_far, 0.0, -1e30)
        key = lax.broadcasted_iota(jnp.int32, (2 * TILE, TILE), 0) + (h * rows + (t - 1) * TILE)
        bias[t, PAD:, :] = jnp.where((key >= begin_of) & (key <= row), 0.0, -1e30)

    @pl.loop(1, trees)
    def _(d):
        held_copy(lax.rem(s + d, trees), s).wait_recv()

    far[h] = held[partner_ref[s]]

    def far_copy(slot, to):
        return send(far.at[slot], far.at[slot], fsend.at[to], frecv.at[slot], head=to)

    for m in range(1, heads):
        far_copy(h, mix(h, m, heads)).start()
    for c in own_copies:
        c.wait()

    @pl.when(h > 0)
    def _():
        for a in range(2):
            halo_copy(a, h).wait_recv()

    for m in range(1, heads):
        far_copy(mix(h, m, heads), h).wait_recv()
    for p in range(heads):
        kx[PROMPT : 2 * PROMPT, p * kw : (p + 1) * kw] = far[p, :, 0:kw]
        vx[PROMPT : 2 * PROMPT, p * kw : (p + 1) * kw] = far[p, :, kw : 2 * kw]

    def part_copy(p, src, i):
        return send(
            pg.at[p * local_kv + i], rg.at[src, i], pgsend.at[p * local_kv + i], pgrecv.at[src, i], head=p
        )

    def strip_copy(j, to):
        return send(hg.at[j], hr.at[j], hgsend.at[j], hgrecv.at[j], head=to)

    def out_copy(j):
        return local(gqv.at[j], gq_hbm.at[:, pl.ds(pl.multiple_of(j * width, width), width)], oq.at[j])

    @pl.loop(0, kv_heads)
    def _(n):
        m = lax.div(n, local_kv)
        i = lax.rem(n, local_kv)
        p = mix(h, m, heads)
        j = p * local_kv + i

        @pl.when(m == 0)
        def _():
            local(
                up_hbm.at[pl.ds(0, rows), pl.ds(0, width)], cot.at[j], cloc.at[i]
            ).wait()

        @pl.when(m > 0)
        def _():
            send(cot.at[j], cot.at[j], csend.at[j], crecv.at[j], head=p).wait_recv()

        cols = pl.ds(pl.multiple_of(j * HEAD_DIM, HEAD_DIM), HEAD_DIM)
        k_prompt, v_prompt = kx[0:PAD, cols], vx[0:PAD, cols]
        dk_parts = [None] * (tiles + 2)
        dv_parts = [None] * (tiles + 2)

        def add(parts, at, x):
            parts[at] = x if parts[at] is None else parts[at] + x

        for t in range(tiles):
            span = slice(t * TILE, (t + 1) * TILE)
            win = slice(PAD + t * TILE, PAD + (t + 2) * TILE)
            k_win = jnp.concatenate([k_prompt, kx[win, cols]], axis=0)
            v_win = jnp.concatenate([v_prompt, vx[win, cols]], axis=0)
            q4 = jnp.concatenate(
                [
                    qv[span, pl.ds(pl.multiple_of(j * width + g * HEAD_DIM, HEAD_DIM), HEAD_DIM)]
                    for g in range(group)
                ],
                axis=0,
            )
            wt = weight[span, :]
            c4 = jnp.concatenate(
                [
                    (cot[j, span, g * HEAD_DIM : (g + 1) * HEAD_DIM].astype(F32) * wt).astype(BF16)
                    for g in range(group)
                ],
                axis=0,
            )
            bt = bias[t]
            sc = dot(k_win, q4, 1, 1) + jnp.concatenate([bt] * group, axis=1)
            top = jnp.max(sc, axis=0, keepdims=True)
            e = jnp.exp2((sc - top) * (scaling * math.log2(math.e)))
            prob = e * (1.0 / jnp.sum(e, axis=0, keepdims=True))
            gp = dot(v_win, c4, 1, 1)
            inner = jnp.sum(prob * gp, axis=0, keepdims=True)
            ds_low = (prob * (gp - inner)).astype(BF16)
            dv = dot(prob.astype(BF16), c4, 1, 0)
            dk = dot(ds_low, q4, 1, 0)
            dq = (dot(k_win, ds_low, 0, 0) * scaling).T
            for g in range(group):
                gqv[j, span, g * HEAD_DIM : (g + 1) * HEAD_DIM] = dq[g * TILE : (g + 1) * TILE].astype(BF16)
            add(dk_parts, 0, dk[0:PAD])
            add(dv_parts, 0, dv[0:PAD])
            for u in range(2):
                add(dk_parts, 1 + t + u, dk[PAD + u * TILE : PAD + (u + 1) * TILE])
                add(dv_parts, 1 + t + u, dv[PAD + u * TILE : PAD + (u + 1) * TILE])
        out_copy(j).start()
        both = [
            jnp.concatenate([a * scaling, b], axis=1) for a, b in zip(dk_parts, dv_parts)
        ]

        @pl.when(m == 0)
        def _():
            pf[i] = both[0][0 : 2 * PROMPT]

        @pl.when(m > 0)
        def _():
            pg[j] = both[0][0 : 2 * PROMPT].astype(BF16)
            part_copy(p, h, i).start()

        @pl.when(h > 0)
        def _():
            hg[j] = both[1].astype(BF16)
            strip_copy(j, h - 1).start()

        for t in range(tiles):
            acc[j, t * TILE : (t + 1) * TILE, :] = both[2 + t]

    for m in range(1, heads):
        p = mix(h, m, heads)
        for i in range(local_kv):
            part_copy(h, p, i).wait_recv()
    for i in range(local_kv):
        total = pf[i]
        for m in range(1, heads):
            total = total + rg[mix(h, m, heads), i].astype(F32)
        pf[i] = total
        back[s, :, i * 256 : (i + 1) * 256] = total[PROMPT : 2 * PROMPT].astype(BF16)

    def back_copy(slot, to):
        return send(back.at[slot], back.at[slot], bsend.at[to], brecv.at[slot], seq=to)

    @pl.loop(1, trees)
    def _(d):
        back_copy(s, lax.rem(s + d, trees)).start()

    @pl.when(h < heads - 1)
    def _():
        for j in range(kv_heads):
            strip_copy(j, h).wait_recv()
            acc[j, rows - HALO : rows, :] = acc[j, rows - HALO : rows, :] + hr[j].astype(F32)

    for j in range(kv_heads):
        gkv[:, j * HEAD_DIM : (j + 1) * HEAD_DIM] = acc[j, :, 0:HEAD_DIM].astype(BF16)
        gvv[:, j * HEAD_DIM : (j + 1) * HEAD_DIM] = acc[j, :, HEAD_DIM:].astype(BF16)

    @pl.loop(1, trees)
    def _(d):
        back_copy(lax.rem(s + d, trees), s).wait_recv()

    arrived = back[partner_ref[s]].astype(F32)
    for i in range(local_kv):
        fout[:, i * 256 : (i + 1) * 256] = (
            pf[i, 0:PROMPT, :] + arrived[:, i * 256 : (i + 1) * 256]
        ).astype(BF16)

    def fin_copy(slot):
        return send(fout, fin.at[slot], finsend.at[0], finrecv.at[slot], head=0)

    @pl.when(h > 0)
    def _():
        fin_copy(h).start()

    @pl.when(h == 0)
    def _():
        for p in range(heads):
            if p > 0:
                fin_copy(p).wait_recv()
            for i in range(local_kv):
                j = p * local_kv + i
                piece = fout[:, i * 256 : (i + 1) * 256] if p == 0 else fin[p, :, i * 256 : (i + 1) * 256]
                gkv[0:PROMPT, j * HEAD_DIM : (j + 1) * HEAD_DIM] = piece[:, 0:HEAD_DIM]
                gvv[0:PROMPT, j * HEAD_DIM : (j + 1) * HEAD_DIM] = piece[:, HEAD_DIM:]

    last = [local(gkv, gk_hbm, okv.at[0]), local(gvv, gv_hbm, okv.at[1])]
    for c in last:
        c.start()

    @pl.when(h == 0)
    def _():
        for to in range(1, heads):
            for a in range(2):
                prompt_copy(a, to).wait_send()

    @pl.when(h < heads - 1)
    def _():
        for a in range(2):
            halo_copy(a, h + 1).wait_send()

    for m in range(1, heads):
        p = mix(h, m, heads)
        far_copy(h, p).wait_send()
        for i in range(local_kv):
            cot_copy(m, i).wait_send()
            part_copy(p, h, i).wait_send()

    @pl.loop(1, trees)
    def _(d):
        to = lax.rem(s + d, trees)
        held_copy(s, to).wait_send()
        back_copy(s, to).wait_send()

    @pl.when(h > 0)
    def _():
        for j in range(kv_heads):
            strip_copy(j, h - 1).wait_send()
        fin_copy(h).wait_send()

    for j in range(kv_heads):
        out_copy(j).wait()
    for c in last:
        c.wait()


def solution(mesh):
    heads, trees = mesh.shape["head"], mesh.shape["seq"]

    def step(queries, keys, values, upstream, lengths, guests, advantage, partner):
        rows, q_width = queries.shape
        kv_width = keys.shape[1]
        kv_heads = kv_width // HEAD_DIM
        group = q_width // kv_width
        local_kv = kv_heads // heads
        width = group * HEAD_DIM
        ext = PAD + HALO + rows
        tiles = rows // TILE
        win = PAD + 2 * TILE
        dma = pltpu.SemaphoreType.DMA
        scratch = [
            pltpu.VMEM((rows, q_width), BF16),
            pltpu.VMEM((kv_heads, rows, width), BF16),
            pltpu.VMEM((ext, kv_width), BF16),
            pltpu.VMEM((ext, kv_width), BF16),
            pltpu.VMEM((tiles, win, TILE), F32),
            pltpu.VMEM((rows, HEAD_DIM), F32),
            pltpu.VMEM((trees, PROMPT, 2 * local_kv * HEAD_DIM), BF16),
            pltpu.VMEM((heads, PROMPT, 2 * local_kv * HEAD_DIM), BF16),
            pltpu.VMEM((kv_heads, rows, width), BF16),
            pltpu.VMEM((kv_heads, 2 * PROMPT, 256), BF16),
            pltpu.VMEM((local_kv, 2 * PROMPT, 256), F32),
            pltpu.VMEM((heads, local_kv, 2 * PROMPT, 256), BF16),
            pltpu.VMEM((kv_heads, HALO, 256), BF16),
            pltpu.VMEM((kv_heads, HALO, 256), BF16),
            pltpu.VMEM((kv_heads, rows, 256), F32),
            pltpu.VMEM((trees, PROMPT, local_kv * 256), BF16),
            pltpu.VMEM((heads, PROMPT, local_kv * 256), BF16),
            pltpu.VMEM((PROMPT, local_kv * 256), BF16),
            pltpu.VMEM((rows, kv_width), BF16),
            pltpu.VMEM((rows, kv_width), BF16),
            dma((5,)), dma((local_kv,)), dma((kv_heads,)), dma((kv_heads,)),
            dma((2,)), dma((2,)), dma((2, heads)), dma((2,)),
            dma((trees,)), dma((trees,)), dma((heads,)), dma((heads,)),
            dma((kv_heads,)), dma((heads, local_kv)), dma((kv_heads,)), dma((kv_heads,)),
            dma((trees,)), dma((trees,)), dma((1,)), dma((heads,)), dma((kv_heads,)), dma((2,)),
        ]
        smem = pl.BlockSpec(memory_space=pltpu.SMEM)
        anywhere = pl.BlockSpec(memory_space=pl.ANY)
        return pl.pallas_call(
            functools.partial(kernel, heads, trees, kv_heads, group, lengths.shape[1]),
            out_shape=(
                jax.ShapeDtypeStruct(queries.shape, BF16),
                jax.ShapeDtypeStruct(keys.shape, BF16),
                jax.ShapeDtypeStruct(values.shape, BF16),
            ),
            in_specs=[smem] * 4 + [anywhere] * 4,
            out_specs=(anywhere,) * 3,
            scratch_shapes=scratch,
            compiler_params=pltpu.CompilerParams(
                collective_id=0, has_side_effects=True, vmem_limit_bytes=56 * 1024 * 1024
            ),
        )(lengths, guests, advantage, partner, queries, keys, values, upstream)

    return jax.shard_map(
        step,
        mesh=mesh,
        in_specs=(
            P(("seq", "head"), None),
            P(("seq", "head"), None),
            P(("seq", "head"), None),
            P("seq", "head"),
            P("seq", None),
            P("seq", None),
            P("seq", None),
            P(),
        ),
        out_specs=(P(("seq", "head"), None), P(("seq", "head"), None), P(("seq", "head"), None)),
        check_vma=False,
    )
```

```python
import functools
import math

import jax
import jax.numpy as jnp
from jax import lax
from jax.experimental import pallas as pl
from jax.experimental.pallas import tpu as pltpu
from jax.sharding import PartitionSpec as P

HEAD_DIM = 128
PROMPT = 48
RESP_LEN = 122
TILE = 128
PAD = 128
HALO = 128
LOGICAL = pl.DeviceIdType.MESH
BF16 = jnp.bfloat16
F32 = jnp.float32


def mix(a, b, size):
    out = 0
    bit = 1
    while bit < size:
        out = out + lax.rem(lax.div(a, bit) + lax.div(b, bit), 2) * bit
        bit *= 2
    return out


def dot(a, b, da, db):
    return lax.dot_general(a, b, (((da,), (db,)), ((), ())), preferred_element_type=F32)


def kernel(
    heads, trees, kv_heads, group, resp,
    len_ref, guest_ref, adv_ref, partner_ref,
    q_hbm, k_hbm, v_hbm, up_hbm,
    gq_hbm, gk_hbm, gv_hbm,
    qv, cot, kx, vx, bias, weight, gqv, pg, pf, rg, hg, hr, acc, fin, fout, gkv, gvv,
    there, there_mid, there_pick, there_out, far, back, back_mid, back_pick, back_out,
    loc, cloc, csend, crecv, hsend, hrecv, psend, precv, fsend, frecv,
    pgsend, pgrecv, hgsend, hgrecv, finsend, finrecv, oq, okv, there_sems, back_sems,
):
    h = lax.axis_index("head")
    s = lax.axis_index("seq")
    rows = q_hbm.shape[0]
    tiles = rows // TILE
    local_kv = kv_heads // heads
    width = group * HEAD_DIM
    half = kv_heads // 2
    pieces = 2 * half
    stride = trees // pieces
    core = lax.rem(h, 2)
    mate = h + 1 - 2 * core
    need = max((rows * b - PROMPT) % RESP_LEN for b in range(1, heads))
    need = -(-need // 16) * 16
    scaling = HEAD_DIM ** (-0.5)

    def send(src, dst, ssem, rsem, **where):
        return pltpu.make_async_remote_copy(
            src_ref=src, dst_ref=dst, send_sem=ssem, recv_sem=rsem, device_id=where, device_id_type=LOGICAL
        )

    def local(src, dst, sem):
        return pltpu.make_async_copy(src, dst, sem)

    own_copies = [
        local(k_hbm, kx.at[pl.ds(PAD + HALO, rows)], loc.at[0]),
        local(v_hbm, vx.at[pl.ds(PAD + HALO, rows)], loc.at[1]),
        local(q_hbm, qv, loc.at[2]),
    ]
    own_prompt = [
        local(k_hbm.at[pl.ds(0, PROMPT)], kx.at[pl.ds(0, PROMPT)], loc.at[3]),
        local(v_hbm.at[pl.ds(0, PROMPT)], vx.at[pl.ds(0, PROMPT)], loc.at[4]),
    ]
    own_cot = [
        local(
            up_hbm.at[pl.ds(pl.multiple_of(h * rows, TILE), rows), pl.ds(i * width, width)],
            cot.at[h * local_kv + i],
            cloc.at[i],
        )
        for i in range(local_kv)
    ]

    barrier = pltpu.get_barrier_semaphore()
    for m in range(1, heads):
        pl.semaphore_signal(barrier, inc=1, device_id={"head": mix(h, m, heads)}, device_id_type=LOGICAL)

    @pl.loop(1, trees)
    def _(d):
        pl.semaphore_signal(barrier, inc=1, device_id={"seq": lax.rem(s + d, trees)}, device_id_type=LOGICAL)

    @pl.when(h == 0)
    def _():
        for c in own_prompt:
            c.start()

    for c in own_copies + own_cot:
        c.start()
    pl.semaphore_wait(barrier, heads + trees - 2)

    def prompt_copy(a, to):
        src, dst = ((k_hbm, kx), (v_hbm, vx))[a]
        return send(
            src.at[pl.ds(0, PROMPT)], dst.at[pl.ds(0, PROMPT)], psend.at[a, to], precv.at[a], head=to
        )

    def halo_copy(a, to):
        src, dst = ((k_hbm, kx), (v_hbm, vx))[a]
        return send(
            src.at[pl.ds(rows - need, need)], dst.at[pl.ds(PAD + HALO - need, need)], hsend.at[a], hrecv.at[a],
            head=to,
        )

    def cot_copy(m, i):
        p = mix(h, m, heads)
        return send(
            up_hbm.at[pl.ds(pl.multiple_of(p * rows, TILE), rows), pl.ds(i * width, width)],
            cot.at[h * local_kv + i],
            csend.at[m * local_kv + i],
            crecv.at[h * local_kv + i],
            head=p,
        )

    def pass_on(a):
        dst = (kx, vx)[a].at[pl.ds(0, PROMPT)]
        return send(dst, dst, psend.at[a, 0], precv.at[a], head=h + 1)

    first_hop = [1] + list(range(2, heads, 2))

    @pl.when(h == 0)
    def _():
        for to in reversed(first_hop):
            for a in range(2):
                prompt_copy(a, to).start()

    @pl.when(h < heads - 1)
    def _():
        for a in range(2):
            halo_copy(a, h + 1).start()

    n_far = (heads - 2) * local_kv

    def far_chunk(n):
        return cot_copy(2 + lax.div(n, local_kv), lax.rem(n, local_kv))

    for i in range(local_kv):
        cot_copy(1, i).start()
    for n in range(min(2, n_far)):
        far_chunk(jnp.int32(n)).start()

    zero_pad = jnp.zeros((PAD - 2 * PROMPT, kx.shape[1]), BF16)
    kx[pl.ds(2 * PROMPT, PAD - 2 * PROMPT), :] = zero_pad
    vx[pl.ds(2 * PROMPT, PAD - 2 * PROMPT), :] = zero_pad

    if need < HALO:
        zero_rest = jnp.zeros((HALO - need, kx.shape[1]), BF16)
        kx[pl.ds(PAD, HALO - need), :] = zero_rest
        vx[pl.ds(PAD, HALO - need), :] = zero_rest

    @pl.when(h == 0)
    def _():
        zero_halo = jnp.zeros((need, kx.shape[1]), BF16)
        kx[pl.ds(PAD + HALO - need, need), :] = zero_halo
        vx[pl.ds(PAD + HALO - need, need), :] = zero_halo
        for c in own_prompt:
            c.wait()

    @pl.when(h > 0)
    def _():
        for a in range(2):
            prompt_copy(a, h).wait_recv()

    @pl.when((h > 1) & (core == 0))
    def _():
        for a in range(2):
            pass_on(a).start()

    def to_middle(bufs, sems, q):
        out, mid, _, _ = bufs
        return send(out.at[q], mid.at[s], sems.at[0, q], sems.at[1, s], seq=q * stride)

    def from_middle(bufs, sems, d):
        _, _, pick, done = bufs
        q = lax.div(s, stride)
        return send(pick.at[d], done.at[q], sems.at[2, d], sems.at[3, q], seq=d)

    def start_exchange(bufs, sems):
        out, mid, _, _ = bufs
        for q in range(pieces):

            @pl.when(s != q * stride)
            def _():
                to_middle(bufs, sems, q).start()

            @pl.when(s == q * stride)
            def _():
                mid[s] = out[q]

    def turn_exchange(bufs, sems):
        out, mid, pick, done = bufs

        @pl.when(lax.rem(s, stride) == 0)
        def _():
            @pl.loop(1, trees)
            def _(d):
                t = lax.rem(s + d, trees)
                send(out.at[0], mid.at[t], sems.at[0, 0], sems.at[1, t], seq=t).wait_recv()

            @pl.loop(1, trees)
            def _(d):
                t = lax.rem(s + d, trees)
                pick[t] = mid[partner_ref[t]]
                from_middle(bufs, sems, t).start()

            done[lax.div(s, stride)] = mid[partner_ref[s]]

    def finish_exchange(bufs, sems):
        _, _, pick, done = bufs
        for q in range(pieces):

            @pl.when(s != q * stride)
            def _():
                send(pick.at[0], done.at[q], sems.at[2, 0], sems.at[3, q], seq=q * stride).wait_recv()

    def sent_exchange(bufs, sems):
        for q in range(pieces):

            @pl.when(s != q * stride)
            def _():
                to_middle(bufs, sems, q).wait_send()

        @pl.when(lax.rem(s, stride) == 0)
        def _():
            @pl.loop(1, trees)
            def _(d):
                from_middle(bufs, sems, lax.rem(s + d, trees)).wait_send()

    there_bufs = (there, there_mid, there_pick, there_out)
    back_bufs = (back, back_mid, back_pick, back_out)

    def lanes(side, i):
        return pl.ds(pl.multiple_of((side * half + i) * HEAD_DIM, HEAD_DIM), HEAD_DIM)

    for i in range(half):
        there[i] = kx[0:PROMPT, lanes(core, i)]
        there[half + i] = vx[0:PROMPT, lanes(core, i)]
    start_exchange(there_bufs, there_sems)

    row_w = lax.broadcasted_iota(jnp.int32, (rows, HEAD_DIM), 0) + h * rows
    w = jnp.ones((rows, HEAD_DIM), F32)
    for r in range(resp):
        begin = PROMPT + r * RESP_LEN
        inside = (row_w >= begin) & (row_w < begin + RESP_LEN)
        w = jnp.where(inside, jnp.where(row_w - begin < len_ref[0, r], adv_ref[0, r], 0.0), w)
    weight[...] = w
    turn_exchange(there_bufs, there_sems)
    for t in range(tiles):
        row = lax.broadcasted_iota(jnp.int32, (8, TILE), 1) + (h * rows + t * TILE)
        begin_of = jnp.full((8, TILE), 1 << 20, jnp.int32)
        guest = jnp.zeros((8, TILE), jnp.int32)
        for r in range(resp):
            begin = PROMPT + r * RESP_LEN
            inside = (row >= begin) & (row < begin + RESP_LEN)
            begin_of = jnp.where(inside, begin, begin_of)
            guest = jnp.where(inside, guest_ref[0, r], guest)
        row, begin_of, guest = row[0:1], begin_of[0:1], guest[0:1]
        col = lax.broadcasted_iota(jnp.int32, (PAD, TILE), 0)
        seen_own = (col < PROMPT) & (guest == 0) & (col <= row)
        seen_far = (col >= PROMPT) & (col < 2 * PROMPT) & (guest == 1)
        bias[t, 0:PAD, :] = jnp.where(seen_own | seen_far, 0.0, -1e30)
        key = lax.broadcasted_iota(jnp.int32, (2 * TILE, TILE), 0) + (h * rows + (t - 1) * TILE)
        bias[t, PAD:, :] = jnp.where((key >= begin_of) & (key <= row), 0.0, -1e30)

    finish_exchange(there_bufs, there_sems)

    def far_copy():
        return send(there_out, far, fsend.at[0], frecv.at[0], head=mate)

    far_copy().start()
    for c in own_copies:
        c.wait()

    @pl.when(h > 0)
    def _():
        for a in range(2):
            halo_copy(a, h).wait_recv()

    low = slice(PROMPT, 2 * PROMPT)
    for i in range(half):
        kx[low, lanes(core, i)] = there_out[i]
        vx[low, lanes(core, i)] = there_out[half + i]
    far_copy().wait_recv()
    for i in range(half):
        kx[low, lanes(1 - core, i)] = far[i]
        vx[low, lanes(1 - core, i)] = far[half + i]

    def part_copy(j, src, o):
        return send(
            pg.at[j], rg.at[src, lax.rem(j, half)], pgsend.at[j], pgrecv.at[src, lax.rem(j, half)], head=o
        )

    def part_arrival(src, i):
        return send(pg.at[0], rg.at[src, i], pgsend.at[0], pgrecv.at[src, i], head=src)

    def strip_copy(j, to):
        return send(
            hg.at[j, pl.ds(HALO - need, need)], hr.at[j], hgsend.at[j], hgrecv.at[j], head=to
        )

    def out_copy(j):
        return local(gqv.at[j], gq_hbm.at[:, pl.ds(pl.multiple_of(j * width, width), width)], oq.at[j])

    @pl.loop(0, kv_heads)
    def _(n):
        m = lax.div(n, local_kv)
        i = lax.rem(n, local_kv)
        p = mix(h, m, heads)
        j = p * local_kv + i

        @pl.when(m == 0)
        def _():
            local(
                up_hbm.at[pl.ds(0, rows), pl.ds(0, width)], cot.at[j], cloc.at[i]
            ).wait()

        @pl.when(m > 0)
        def _():
            send(cot.at[j], cot.at[j], csend.at[j], crecv.at[j], head=p).wait_recv()

        cols = pl.ds(pl.multiple_of(j * HEAD_DIM, HEAD_DIM), HEAD_DIM)
        k_prompt, v_prompt = kx[0:PAD, cols], vx[0:PAD, cols]
        dk_parts = [None] * (tiles + 2)
        dv_parts = [None] * (tiles + 2)

        def add(parts, at, x):
            parts[at] = x if parts[at] is None else parts[at] + x

        for t in range(tiles):
            span = slice(t * TILE, (t + 1) * TILE)
            win = slice(PAD + t * TILE, PAD + (t + 2) * TILE)
            k_win = jnp.concatenate([k_prompt, kx[win, cols]], axis=0)
            v_win = jnp.concatenate([v_prompt, vx[win, cols]], axis=0)
            q4 = jnp.concatenate(
                [
                    qv[span, pl.ds(pl.multiple_of(j * width + g * HEAD_DIM, HEAD_DIM), HEAD_DIM)]
                    for g in range(group)
                ],
                axis=0,
            )
            wt = weight[span, :]
            c4 = jnp.concatenate(
                [
                    (cot[j, span, g * HEAD_DIM : (g + 1) * HEAD_DIM].astype(F32) * wt).astype(BF16)
                    for g in range(group)
                ],
                axis=0,
            )
            bt = bias[t]
            sc = dot(k_win, q4, 1, 1) + jnp.concatenate([bt] * group, axis=1)
            top = jnp.max(sc, axis=0, keepdims=True)
            e = jnp.exp2((sc - top) * (scaling * math.log2(math.e)))
            prob = e * (1.0 / jnp.sum(e, axis=0, keepdims=True))
            gp = dot(v_win, c4, 1, 1)
            inner = jnp.sum(prob * gp, axis=0, keepdims=True)
            ds_low = (prob * (gp - inner)).astype(BF16)
            dv = dot(prob.astype(BF16), c4, 1, 0)
            dk = dot(ds_low, q4, 1, 0)
            dq = (dot(k_win, ds_low, 0, 0) * scaling).T
            for g in range(group):
                gqv[j, span, g * HEAD_DIM : (g + 1) * HEAD_DIM] = dq[g * TILE : (g + 1) * TILE].astype(BF16)
            add(dk_parts, 0, dk[0:PAD])
            add(dv_parts, 0, dv[0:PAD])
            for u in range(2):
                add(dk_parts, 1 + t + u, dk[PAD + u * TILE : PAD + (u + 1) * TILE])
                add(dv_parts, 1 + t + u, dv[PAD + u * TILE : PAD + (u + 1) * TILE])
        out_copy(j).start()
        both = [
            jnp.concatenate([a * scaling, b], axis=1) for a, b in zip(dk_parts, dv_parts)
        ]

        owner = lax.div(j, half)

        @pl.when(h == owner)
        def _():
            pf[lax.rem(j, half)] = both[0][0 : 2 * PROMPT]

        @pl.when(h != owner)
        def _():
            pg[j] = both[0][0 : 2 * PROMPT].astype(BF16)
            part_copy(j, h, owner).start()

        @pl.when(h > 0)
        def _():
            hg[j] = both[1].astype(BF16)
            strip_copy(j, h - 1).start()

        for t in range(tiles):
            acc[j, t * TILE : (t + 1) * TILE, :] = both[2 + t]

        @pl.when(n < n_far - 2)
        def _():
            far_chunk(n).wait_send()
            far_chunk(n + 2).start()

    @pl.when(h < 2)
    def _():
        for i in range(half):
            total = pf[i]
            for m in range(1, heads):
                part_arrival(mix(h, m, heads), i).wait_recv()
                total = total + rg[mix(h, m, heads), i].astype(F32)
            pf[i] = total
            back[i] = total[low, 0:HEAD_DIM].astype(BF16)
            back[half + i] = total[low, HEAD_DIM:].astype(BF16)
        start_exchange(back_bufs, back_sems)
        turn_exchange(back_bufs, back_sems)

    @pl.when(h < heads - 1)
    def _():
        for j in range(kv_heads):
            strip_copy(j, h).wait_recv()
            acc[j, rows - need : rows, :] = acc[j, rows - need : rows, :] + hr[j].astype(F32)

    for j in range(kv_heads):
        gkv[:, j * HEAD_DIM : (j + 1) * HEAD_DIM] = acc[j, :, 0:HEAD_DIM].astype(BF16)
        gvv[:, j * HEAD_DIM : (j + 1) * HEAD_DIM] = acc[j, :, HEAD_DIM:].astype(BF16)

    def rows_out(a, begin, count, at):
        src, dst = ((gkv, gk_hbm), (gvv, gv_hbm))[a]
        return local(src.at[pl.ds(begin, count)], dst.at[pl.ds(begin, count)], okv.at[at])

    last = [rows_out(a, PROMPT, rows - PROMPT, a) for a in range(2)]
    top_rows = [rows_out(a, 0, PROMPT, 2 + a) for a in range(2)]
    for c in last:
        c.start()

    def fin_copy():
        return send(fout, fin, finsend.at[0], finrecv.at[0], head=0)

    @pl.when(h < 2)
    def _():
        finish_exchange(back_bufs, back_sems)
        for i in range(half):
            fout[i] = (pf[i, 0:PROMPT, 0:HEAD_DIM] + back_out[i].astype(F32)).astype(BF16)
            fout[half + i] = (pf[i, 0:PROMPT, HEAD_DIM:] + back_out[half + i].astype(F32)).astype(BF16)

    @pl.when(h == 1)
    def _():
        fin_copy().start()

    @pl.when(h == 0)
    def _():
        for o in range(2):
            if o == 1:
                send(fout, fin, finsend.at[0], finrecv.at[0], head=1).wait_recv()
            piece = (fout, fin)[o]
            for i in range(half):
                at = (o * half + i) * HEAD_DIM
                gkv[0:PROMPT, at : at + HEAD_DIM] = piece[i]
                gvv[0:PROMPT, at : at + HEAD_DIM] = piece[half + i]

    for c in top_rows:
        c.start()

    @pl.when(h == 0)
    def _():
        for to in first_hop:
            for a in range(2):
                prompt_copy(a, to).wait_send()

    @pl.when((h > 1) & (core == 0))
    def _():
        for a in range(2):
            pass_on(a).wait_send()

    @pl.when(h < heads - 1)
    def _():
        for a in range(2):
            halo_copy(a, h + 1).wait_send()

    for i in range(local_kv):
        cot_copy(1, i).wait_send()
    for n in range(max(0, n_far - 2), n_far):
        far_chunk(jnp.int32(n)).wait_send()
    far_copy().wait_send()
    sent_exchange(there_bufs, there_sems)
    for j in range(kv_heads):
        o = j // half

        @pl.when(h != o)
        def _():
            part_copy(jnp.int32(j), h, o).wait_send()

    @pl.when(h < 2)
    def _():
        sent_exchange(back_bufs, back_sems)

    @pl.when(h > 0)
    def _():
        for j in range(kv_heads):
            strip_copy(j, h - 1).wait_send()

    @pl.when(h == 1)
    def _():
        fin_copy().wait_send()

    for j in range(kv_heads):
        out_copy(j).wait()
    for c in last + top_rows:
        c.wait()


def hand_over(gq, gk, gv, gq_out, gk_out, gv_out, sems):
    copies = []
    for src, dst, parts in ((gq, gq_out, 8), (gk, gk_out, 2), (gv, gv_out, 2)):
        size = src.shape[0] // parts
        for i in range(parts):
            at = pl.ds(i * size, size)
            copies.append(pltpu.make_async_copy(src.at[at], dst.at[at], sems.at[len(copies)]))
    for c in copies:
        c.start()
    for c in copies:
        c.wait()


def solution(mesh):
    heads, trees = mesh.shape["head"], mesh.shape["seq"]

    def step(queries, keys, values, upstream, lengths, guests, advantage, partner):
        rows, q_width = queries.shape
        kv_width = keys.shape[1]
        kv_heads = kv_width // HEAD_DIM
        group = q_width // kv_width
        local_kv = kv_heads // heads
        half = kv_heads // 2
        need = max((rows * b - PROMPT) % RESP_LEN for b in range(1, heads))
        need = -(-need // 16) * 16
        width = group * HEAD_DIM
        ext = PAD + HALO + rows
        tiles = rows // TILE
        win = PAD + 2 * TILE
        dma = pltpu.SemaphoreType.DMA
        scratch = [
            pltpu.VMEM((rows, q_width), BF16),
            pltpu.VMEM((kv_heads, rows, width), BF16),
            pltpu.VMEM((ext, kv_width), BF16),
            pltpu.VMEM((ext, kv_width), BF16),
            pltpu.VMEM((tiles, win, TILE), F32),
            pltpu.VMEM((rows, HEAD_DIM), F32),
            pltpu.VMEM((kv_heads, rows, width), BF16),
            pltpu.VMEM((kv_heads, 2 * PROMPT, 256), BF16),
            pltpu.VMEM((half, 2 * PROMPT, 256), F32),
            pltpu.VMEM((heads, half, 2 * PROMPT, 256), BF16),
            pltpu.VMEM((kv_heads, HALO, 256), BF16),
            pltpu.VMEM((kv_heads, need, 256), BF16),
            pltpu.VMEM((kv_heads, rows, 256), F32),
            pltpu.VMEM((2 * half, PROMPT, HEAD_DIM), BF16),
            pltpu.VMEM((2 * half, PROMPT, HEAD_DIM), BF16),
            pltpu.VMEM((rows, kv_width), BF16),
            pltpu.VMEM((rows, kv_width), BF16),
            *[pltpu.VMEM((n, PROMPT, HEAD_DIM), BF16) for n in (2 * half, trees, trees, 2 * half, 2 * half)],
            *[pltpu.VMEM((n, PROMPT, HEAD_DIM), BF16) for n in (2 * half, trees, trees, 2 * half)],
            dma((5,)), dma((local_kv,)), dma((kv_heads,)), dma((kv_heads,)),
            dma((2,)), dma((2,)), dma((2, heads)), dma((2,)), dma((1,)), dma((1,)),
            dma((kv_heads,)), dma((heads, half)), dma((kv_heads,)), dma((kv_heads,)),
            dma((1,)), dma((1,)), dma((kv_heads,)), dma((4,)),
            dma((4, max(trees, 2 * half))), dma((4, max(trees, 2 * half))),
        ]
        smem = pl.BlockSpec(memory_space=pltpu.SMEM)
        anywhere = pl.BlockSpec(memory_space=pl.ANY)
        grads = pl.pallas_call(
            functools.partial(kernel, heads, trees, kv_heads, group, lengths.shape[1]),
            out_shape=(
                jax.ShapeDtypeStruct(queries.shape, BF16),
                jax.ShapeDtypeStruct(keys.shape, BF16),
                jax.ShapeDtypeStruct(values.shape, BF16),
            ),
            in_specs=[smem] * 4 + [anywhere] * 4,
            out_specs=(anywhere,) * 3,
            scratch_shapes=scratch,
            compiler_params=pltpu.CompilerParams(
                collective_id=0, has_side_effects=True, vmem_limit_bytes=56 * 1024 * 1024
            ),
        )(lengths, guests, advantage, partner, queries, keys, values, upstream)
        return pl.pallas_call(
            hand_over,
            out_shape=tuple(jax.ShapeDtypeStruct(x.shape, x.dtype) for x in grads),
            in_specs=[anywhere] * 3,
            out_specs=(anywhere,) * 3,
            scratch_shapes=[dma((12,))],
        )(*grads)

    return jax.shard_map(
        step,
        mesh=mesh,
        in_specs=(
            P(("seq", "head"), None),
            P(("seq", "head"), None),
            P(("seq", "head"), None),
            P("seq", "head"),
            P("seq", None),
            P("seq", None),
            P("seq", None),
            P(),
        ),
        out_specs=(P(("seq", "head"), None), P(("seq", "head"), None), P(("seq", "head"), None)),
        check_vma=False,
    )
```

```python
import functools
import math

import jax
import jax.numpy as jnp
from jax import lax
from jax.experimental import pallas as pl
from jax.experimental.pallas import tpu as pltpu
from jax.sharding import PartitionSpec as P

HEAD_DIM = 128
PROMPT = 48
RESP_LEN = 122
TILE = 128
PAD = 128
HALO = 128
LOGICAL = pl.DeviceIdType.MESH
BF16 = jnp.bfloat16
F32 = jnp.float32


def mix(a, b, size):
    out = 0
    bit = 1
    while bit < size:
        out = out + lax.rem(lax.div(a, bit) + lax.div(b, bit), 2) * bit
        bit *= 2
    return out


def dot(a, b, da, db):
    return lax.dot_general(a, b, (((da,), (db,)), ((), ())), preferred_element_type=F32)


def kernel(
    heads, trees, kv_heads, group, resp,
    len_ref, guest_ref, adv_ref, partner_ref,
    q_hbm, k_hbm, v_hbm, up_hbm,
    gq_hbm, gk_hbm, gv_hbm,
    qv, cot, kx, vx, bias, weight, seen_scores, seen_top, gqv, pg, pf, rg, hg, hr, acc, fin, fout, gkv, gvv,
    there, there_mid, there_pick, there_out, far, back, back_mid, back_pick, back_out,
    loc, cloc, csend, crecv, hsend, hrecv, psend, precv, fsend, frecv,
    pgsend, pgrecv, hgsend, hgrecv, finsend, finrecv, oq, okv, there_sems, back_sems,
):
    h = lax.axis_index("head")
    s = lax.axis_index("seq")
    rows = q_hbm.shape[0]
    tiles = rows // TILE
    local_kv = kv_heads // heads
    width = group * HEAD_DIM
    half = kv_heads // 2
    pieces = 2 * half
    stride = trees // pieces
    core = lax.rem(h, 2)
    mate = h + 1 - 2 * core
    need = max((rows * b - PROMPT) % RESP_LEN for b in range(1, heads))
    need = -(-need // 16) * 16
    scaling = HEAD_DIM ** (-0.5)

    def send(src, dst, ssem, rsem, **where):
        return pltpu.make_async_remote_copy(
            src_ref=src, dst_ref=dst, send_sem=ssem, recv_sem=rsem, device_id=where, device_id_type=LOGICAL
        )

    def local(src, dst, sem):
        return pltpu.make_async_copy(src, dst, sem)

    own_copies = [
        local(k_hbm, kx.at[pl.ds(PAD + HALO, rows)], loc.at[0]),
        local(v_hbm, vx.at[pl.ds(PAD + HALO, rows)], loc.at[1]),
        local(q_hbm, qv, loc.at[2]),
    ]
    own_prompt = [
        local(k_hbm.at[pl.ds(0, PROMPT)], kx.at[pl.ds(0, PROMPT)], loc.at[3]),
        local(v_hbm.at[pl.ds(0, PROMPT)], vx.at[pl.ds(0, PROMPT)], loc.at[4]),
    ]
    own_cot = [
        local(
            up_hbm.at[pl.ds(pl.multiple_of(h * rows, TILE), rows), pl.ds(i * width, width)],
            cot.at[h * local_kv + i],
            cloc.at[i],
        )
        for i in range(local_kv)
    ]

    barrier = pltpu.get_barrier_semaphore()
    for m in range(1, heads):
        pl.semaphore_signal(barrier, inc=1, device_id={"head": mix(h, m, heads)}, device_id_type=LOGICAL)

    @pl.loop(1, trees)
    def _(d):
        pl.semaphore_signal(barrier, inc=1, device_id={"seq": lax.rem(s + d, trees)}, device_id_type=LOGICAL)

    @pl.when(h == 0)
    def _():
        for c in own_prompt:
            c.start()

    for c in own_copies + own_cot:
        c.start()
    pl.semaphore_wait(barrier, heads + trees - 2)

    def prompt_copy(a, to):
        src, dst = ((k_hbm, kx), (v_hbm, vx))[a]
        return send(
            src.at[pl.ds(0, PROMPT)], dst.at[pl.ds(0, PROMPT)], psend.at[a, to], precv.at[a], head=to
        )

    def halo_copy(a, to):
        src, dst = ((k_hbm, kx), (v_hbm, vx))[a]
        return send(
            src.at[pl.ds(rows - need, need)], dst.at[pl.ds(PAD + HALO - need, need)], hsend.at[a], hrecv.at[a],
            head=to,
        )

    def cot_copy(m, i):
        p = mix(h, m, heads)
        return send(
            up_hbm.at[pl.ds(pl.multiple_of(p * rows, TILE), rows), pl.ds(i * width, width)],
            cot.at[h * local_kv + i],
            csend.at[m * local_kv + i],
            crecv.at[h * local_kv + i],
            head=p,
        )

    def pass_on(a):
        dst = (kx, vx)[a].at[pl.ds(0, PROMPT)]
        return send(dst, dst, psend.at[a, 0], precv.at[a], head=h + 1)

    first_hop = [1] + list(range(2, heads, 2))

    @pl.when(h == 0)
    def _():
        for to in reversed(first_hop):
            for a in range(2):
                prompt_copy(a, to).start()

    @pl.when(h < heads - 1)
    def _():
        for a in range(2):
            halo_copy(a, h + 1).start()

    n_far = (heads - 2) * local_kv

    def far_chunk(n):
        return cot_copy(2 + lax.div(n, local_kv), lax.rem(n, local_kv))

    for i in range(local_kv):
        cot_copy(1, i).start()
    for n in range(min(2, n_far)):
        far_chunk(jnp.int32(n)).start()

    zero_pad = jnp.zeros((PAD - 2 * PROMPT, kx.shape[1]), BF16)
    kx[pl.ds(2 * PROMPT, PAD - 2 * PROMPT), :] = zero_pad
    vx[pl.ds(2 * PROMPT, PAD - 2 * PROMPT), :] = zero_pad

    if need < HALO:
        zero_rest = jnp.zeros((HALO - need, kx.shape[1]), BF16)
        kx[pl.ds(PAD, HALO - need), :] = zero_rest
        vx[pl.ds(PAD, HALO - need), :] = zero_rest

    @pl.when(h == 0)
    def _():
        zero_halo = jnp.zeros((need, kx.shape[1]), BF16)
        kx[pl.ds(PAD + HALO - need, need), :] = zero_halo
        vx[pl.ds(PAD + HALO - need, need), :] = zero_halo
        for c in own_prompt:
            c.wait()

    @pl.when(h > 0)
    def _():
        for a in range(2):
            prompt_copy(a, h).wait_recv()

    @pl.when((h > 1) & (core == 0))
    def _():
        for a in range(2):
            pass_on(a).start()

    def to_middle(bufs, sems, q):
        out, mid, _, _ = bufs
        return send(out.at[q], mid.at[s], sems.at[0, q], sems.at[1, s], seq=q * stride)

    def from_middle(bufs, sems, d):
        _, _, pick, done = bufs
        q = lax.div(s, stride)
        return send(pick.at[d], done.at[q], sems.at[2, d], sems.at[3, q], seq=d)

    def start_exchange(bufs, sems):
        out, mid, _, _ = bufs
        for q in range(pieces):

            @pl.when(s != q * stride)
            def _():
                to_middle(bufs, sems, q).start()

            @pl.when(s == q * stride)
            def _():
                mid[s] = out[q]

    def turn_exchange(bufs, sems):
        out, mid, pick, done = bufs

        @pl.when(lax.rem(s, stride) == 0)
        def _():
            @pl.loop(1, trees)
            def _(d):
                t = lax.rem(s + d, trees)
                send(out.at[0], mid.at[t], sems.at[0, 0], sems.at[1, t], seq=t).wait_recv()

            @pl.loop(1, trees)
            def _(d):
                t = lax.rem(s + d, trees)
                pick[t] = mid[partner_ref[t]]
                from_middle(bufs, sems, t).start()

            done[lax.div(s, stride)] = mid[partner_ref[s]]

    def finish_exchange(bufs, sems):
        _, _, pick, done = bufs
        for q in range(pieces):

            @pl.when(s != q * stride)
            def _():
                send(pick.at[0], done.at[q], sems.at[2, 0], sems.at[3, q], seq=q * stride).wait_recv()

    def sent_exchange(bufs, sems):
        for q in range(pieces):

            @pl.when(s != q * stride)
            def _():
                to_middle(bufs, sems, q).wait_send()

        @pl.when(lax.rem(s, stride) == 0)
        def _():
            @pl.loop(1, trees)
            def _(d):
                from_middle(bufs, sems, lax.rem(s + d, trees)).wait_send()

    there_bufs = (there, there_mid, there_pick, there_out)
    back_bufs = (back, back_mid, back_pick, back_out)

    def lanes(side, i):
        return pl.ds(pl.multiple_of((side * half + i) * HEAD_DIM, HEAD_DIM), HEAD_DIM)

    for i in range(half):
        there[i] = kx[0:PROMPT, lanes(core, i)]
        there[half + i] = vx[0:PROMPT, lanes(core, i)]
    start_exchange(there_bufs, there_sems)

    row_w = lax.broadcasted_iota(jnp.int32, (rows, HEAD_DIM), 0) + h * rows
    w = jnp.ones((rows, HEAD_DIM), F32)
    for r in range(resp):
        begin = PROMPT + r * RESP_LEN
        inside = (row_w >= begin) & (row_w < begin + RESP_LEN)
        w = jnp.where(inside, jnp.where(row_w - begin < len_ref[0, r], adv_ref[0, r], 0.0), w)
    weight[...] = w
    for t in range(tiles):
        row = lax.broadcasted_iota(jnp.int32, (8, TILE), 1) + (h * rows + t * TILE)
        begin_of = jnp.full((8, TILE), 1 << 20, jnp.int32)
        guest = jnp.zeros((8, TILE), jnp.int32)
        for r in range(resp):
            begin = PROMPT + r * RESP_LEN
            inside = (row >= begin) & (row < begin + RESP_LEN)
            begin_of = jnp.where(inside, begin, begin_of)
            guest = jnp.where(inside, guest_ref[0, r], guest)
        row, begin_of, guest = row[0:1], begin_of[0:1], guest[0:1]
        col = lax.broadcasted_iota(jnp.int32, (PAD, TILE), 0)
        seen_own = (col < PROMPT) & (guest == 0) & (col <= row)
        seen_far = (col >= PROMPT) & (col < 2 * PROMPT) & (guest == 1)
        bias[t, 0:PAD, :] = jnp.where(seen_own | seen_far, 0.0, -1e30)
        key = lax.broadcasted_iota(jnp.int32, (2 * TILE, TILE), 0) + (h * rows + (t - 1) * TILE)
        bias[t, PAD:, :] = jnp.where((key >= begin_of) & (key <= row), 0.0, -1e30)

    for c in own_copies:
        c.wait()

    @pl.when(h > 0)
    def _():
        for a in range(2):
            halo_copy(a, h).wait_recv()

    def stacked(j, t):
        return jnp.concatenate(
            [
                qv[
                    t * TILE : (t + 1) * TILE,
                    pl.ds(pl.multiple_of(j * width + g * HEAD_DIM, HEAD_DIM), HEAD_DIM),
                ]
                for g in range(group)
            ],
            axis=0,
        )

    def score_rows(j):
        cols = pl.ds(pl.multiple_of(j * HEAD_DIM, HEAD_DIM), HEAD_DIM)
        for t in range(tiles):
            win = slice(PAD + t * TILE, PAD + (t + 2) * TILE)
            sc = dot(kx[win, cols], stacked(j, t), 1, 1)
            sc = sc + jnp.concatenate([bias[t, PAD:, :]] * group, axis=1)
            seen_scores[j, t] = sc
            seen_top[j, t] = jnp.max(sc, axis=0, keepdims=True)

    @pl.loop(0, kv_heads // 2)
    def _(j):
        score_rows(j)

    turn_exchange(there_bufs, there_sems)

    @pl.loop(kv_heads // 2, kv_heads)
    def _(j):
        score_rows(j)

    finish_exchange(there_bufs, there_sems)

    def far_copy():
        return send(there_out, far, fsend.at[0], frecv.at[0], head=mate)

    far_copy().start()
    low = slice(PROMPT, 2 * PROMPT)
    for i in range(half):
        kx[low, lanes(core, i)] = there_out[i]
        vx[low, lanes(core, i)] = there_out[half + i]
    far_copy().wait_recv()
    for i in range(half):
        kx[low, lanes(1 - core, i)] = far[i]
        vx[low, lanes(1 - core, i)] = far[half + i]

    def part_copy(j, src, o):
        return send(
            pg.at[j], rg.at[src, lax.rem(j, half)], pgsend.at[j], pgrecv.at[src, lax.rem(j, half)], head=o
        )

    def part_arrival(src, i):
        return send(pg.at[0], rg.at[src, i], pgsend.at[0], pgrecv.at[src, i], head=src)

    def strip_copy(j, to):
        return send(
            hg.at[j, pl.ds(HALO - need, need)], hr.at[j], hgsend.at[j], hgrecv.at[j], head=to
        )

    def out_copy(j):
        return local(gqv.at[j], gq_hbm.at[:, pl.ds(pl.multiple_of(j * width, width), width)], oq.at[j])

    @pl.loop(0, kv_heads)
    def _(n):
        m = lax.div(n, local_kv)
        i = lax.rem(n, local_kv)
        p = mix(h, m, heads)
        j = p * local_kv + i

        @pl.when(m == 0)
        def _():
            local(
                up_hbm.at[pl.ds(0, rows), pl.ds(0, width)], cot.at[j], cloc.at[i]
            ).wait()

        @pl.when(m > 0)
        def _():
            send(cot.at[j], cot.at[j], csend.at[j], crecv.at[j], head=p).wait_recv()

        cols = pl.ds(pl.multiple_of(j * HEAD_DIM, HEAD_DIM), HEAD_DIM)
        k_prompt, v_prompt = kx[0:PAD, cols], vx[0:PAD, cols]
        dk_parts = [None] * (tiles + 2)
        dv_parts = [None] * (tiles + 2)

        def add(parts, at, x):
            parts[at] = x if parts[at] is None else parts[at] + x

        for t in range(tiles):
            span = slice(t * TILE, (t + 1) * TILE)
            win = slice(PAD + t * TILE, PAD + (t + 2) * TILE)
            k_win = jnp.concatenate([k_prompt, kx[win, cols]], axis=0)
            v_win = jnp.concatenate([v_prompt, vx[win, cols]], axis=0)
            q4 = stacked(j, t)
            wt = weight[span, :]
            c4 = jnp.concatenate(
                [
                    (cot[j, span, g * HEAD_DIM : (g + 1) * HEAD_DIM].astype(F32) * wt).astype(BF16)
                    for g in range(group)
                ],
                axis=0,
            )
            first = dot(k_prompt, q4, 1, 1) + jnp.concatenate([bias[t, 0:PAD, :]] * group, axis=1)
            top = jnp.maximum(jnp.max(first, axis=0, keepdims=True), seen_top[j, t])
            sc = jnp.concatenate([first, seen_scores[j, t]], axis=0)
            e = jnp.exp2((sc - top) * (scaling * math.log2(math.e)))
            prob = e * (1.0 / jnp.sum(e, axis=0, keepdims=True))
            gp = dot(v_win, c4, 1, 1)
            inner = jnp.sum(prob * gp, axis=0, keepdims=True)
            ds_low = (prob * (gp - inner)).astype(BF16)
            dv = dot(prob.astype(BF16), c4, 1, 0)
            dk = dot(ds_low, q4, 1, 0)
            dq = (dot(k_win, ds_low, 0, 0) * scaling).astype(BF16).T
            for g in range(group):
                gqv[j, span, g * HEAD_DIM : (g + 1) * HEAD_DIM] = dq[g * TILE : (g + 1) * TILE]
            add(dk_parts, 0, dk[0:PAD])
            add(dv_parts, 0, dv[0:PAD])
            for u in range(2):
                add(dk_parts, 1 + t + u, dk[PAD + u * TILE : PAD + (u + 1) * TILE])
                add(dv_parts, 1 + t + u, dv[PAD + u * TILE : PAD + (u + 1) * TILE])
        out_copy(j).start()
        both = [
            jnp.concatenate([a * scaling, b], axis=1) for a, b in zip(dk_parts, dv_parts)
        ]

        owner = lax.div(j, half)

        @pl.when(h == owner)
        def _():
            pf[lax.rem(j, half)] = both[0][0 : 2 * PROMPT]

        @pl.when(h != owner)
        def _():
            pg[j] = both[0][0 : 2 * PROMPT].astype(BF16)
            part_copy(j, h, owner).start()

        @pl.when(h > 0)
        def _():
            hg[j] = both[1].astype(BF16)
            strip_copy(j, h - 1).start()

        for t in range(tiles):
            acc[j, t * TILE : (t + 1) * TILE, :] = both[2 + t]

        @pl.when(n < n_far - 2)
        def _():
            far_chunk(n).wait_send()
            far_chunk(n + 2).start()

    @pl.when(h < 2)
    def _():
        for i in range(half):
            total = pf[i]
            for m in range(1, heads):
                part_arrival(mix(h, m, heads), i).wait_recv()
                total = total + rg[mix(h, m, heads), i].astype(F32)
            pf[i] = total
            back[i] = total[low, 0:HEAD_DIM].astype(BF16)
            back[half + i] = total[low, HEAD_DIM:].astype(BF16)
        start_exchange(back_bufs, back_sems)
        turn_exchange(back_bufs, back_sems)

    @pl.when(h < heads - 1)
    def _():
        for j in range(kv_heads):
            strip_copy(j, h).wait_recv()
            acc[j, rows - need : rows, :] = acc[j, rows - need : rows, :] + hr[j].astype(F32)

    for j in range(kv_heads):
        gkv[:, j * HEAD_DIM : (j + 1) * HEAD_DIM] = acc[j, :, 0:HEAD_DIM].astype(BF16)
        gvv[:, j * HEAD_DIM : (j + 1) * HEAD_DIM] = acc[j, :, HEAD_DIM:].astype(BF16)

    def rows_out(a, begin, count, at):
        src, dst = ((gkv, gk_hbm), (gvv, gv_hbm))[a]
        return local(src.at[pl.ds(begin, count)], dst.at[pl.ds(begin, count)], okv.at[at])

    last = [rows_out(a, PROMPT, rows - PROMPT, a) for a in range(2)]
    top_rows = [rows_out(a, 0, PROMPT, 2 + a) for a in range(2)]
    for c in last:
        c.start()

    def fin_copy():
        return send(fout, fin, finsend.at[0], finrecv.at[0], head=0)

    @pl.when(h < 2)
    def _():
        finish_exchange(back_bufs, back_sems)
        for i in range(half):
            fout[i] = (pf[i, 0:PROMPT, 0:HEAD_DIM] + back_out[i].astype(F32)).astype(BF16)
            fout[half + i] = (pf[i, 0:PROMPT, HEAD_DIM:] + back_out[half + i].astype(F32)).astype(BF16)

    @pl.when(h == 1)
    def _():
        fin_copy().start()

    @pl.when(h == 0)
    def _():
        for o in range(2):
            if o == 1:
                send(fout, fin, finsend.at[0], finrecv.at[0], head=1).wait_recv()
            piece = (fout, fin)[o]
            for i in range(half):
                at = (o * half + i) * HEAD_DIM
                gkv[0:PROMPT, at : at + HEAD_DIM] = piece[i]
                gvv[0:PROMPT, at : at + HEAD_DIM] = piece[half + i]

    for c in top_rows:
        c.start()

    @pl.when(h == 0)
    def _():
        for to in first_hop:
            for a in range(2):
                prompt_copy(a, to).wait_send()

    @pl.when((h > 1) & (core == 0))
    def _():
        for a in range(2):
            pass_on(a).wait_send()

    @pl.when(h < heads - 1)
    def _():
        for a in range(2):
            halo_copy(a, h + 1).wait_send()

    for i in range(local_kv):
        cot_copy(1, i).wait_send()
    for n in range(max(0, n_far - 2), n_far):
        far_chunk(jnp.int32(n)).wait_send()
    far_copy().wait_send()
    sent_exchange(there_bufs, there_sems)
    for j in range(kv_heads):
        o = j // half

        @pl.when(h != o)
        def _():
            part_copy(jnp.int32(j), h, o).wait_send()

    @pl.when(h < 2)
    def _():
        sent_exchange(back_bufs, back_sems)

    @pl.when(h > 0)
    def _():
        for j in range(kv_heads):
            strip_copy(j, h - 1).wait_send()

    @pl.when(h == 1)
    def _():
        fin_copy().wait_send()

    for j in range(kv_heads):
        out_copy(j).wait()
    for c in last + top_rows:
        c.wait()


def hand_over(gq, gk, gv, gq_out, gk_out, gv_out, gq_mid, gk_mid, gv_mid, sems):
    ins, outs = [], []
    for src, mid, dst, parts in ((gq, gq_mid, gq_out, 8), (gk, gk_mid, gk_out, 2), (gv, gv_mid, gv_out, 2)):
        size = src.shape[0] // parts
        for i in range(parts):
            at = pl.ds(i * size, size)
            ins.append(pltpu.make_async_copy(src.at[at], mid.at[at], sems.at[0, len(ins)]))
            outs.append(pltpu.make_async_copy(mid.at[at], dst.at[at], sems.at[1, len(outs)]))
    for c in ins:
        c.start()
    for c, d in zip(ins, outs):
        c.wait()
        d.start()
    for d in outs:
        d.wait()


def solution(mesh):
    heads, trees = mesh.shape["head"], mesh.shape["seq"]

    def step(queries, keys, values, upstream, lengths, guests, advantage, partner):
        rows, q_width = queries.shape
        kv_width = keys.shape[1]
        kv_heads = kv_width // HEAD_DIM
        group = q_width // kv_width
        local_kv = kv_heads // heads
        half = kv_heads // 2
        need = max((rows * b - PROMPT) % RESP_LEN for b in range(1, heads))
        need = -(-need // 16) * 16
        width = group * HEAD_DIM
        ext = PAD + HALO + rows
        tiles = rows // TILE
        win = PAD + 2 * TILE
        dma = pltpu.SemaphoreType.DMA
        scratch = [
            pltpu.VMEM((rows, q_width), BF16),
            pltpu.VMEM((kv_heads, rows, width), BF16),
            pltpu.VMEM((ext, kv_width), BF16),
            pltpu.VMEM((ext, kv_width), BF16),
            pltpu.VMEM((tiles, win, TILE), F32),
            pltpu.VMEM((rows, HEAD_DIM), F32),
            pltpu.VMEM((kv_heads, tiles, 2 * TILE, group * TILE), F32),
            pltpu.VMEM((kv_heads, tiles, 1, group * TILE), F32),
            pltpu.VMEM((kv_heads, rows, width), BF16),
            pltpu.VMEM((kv_heads, 2 * PROMPT, 256), BF16),
            pltpu.VMEM((half, 2 * PROMPT, 256), F32),
            pltpu.VMEM((heads, half, 2 * PROMPT, 256), BF16),
            pltpu.VMEM((kv_heads, HALO, 256), BF16),
            pltpu.VMEM((kv_heads, need, 256), BF16),
            pltpu.VMEM((kv_heads, rows, 256), F32),
            pltpu.VMEM((2 * half, PROMPT, HEAD_DIM), BF16),
            pltpu.VMEM((2 * half, PROMPT, HEAD_DIM), BF16),
            pltpu.VMEM((rows, kv_width), BF16),
            pltpu.VMEM((rows, kv_width), BF16),
            *[pltpu.VMEM((n, PROMPT, HEAD_DIM), BF16) for n in (2 * half, trees, trees, 2 * half, 2 * half)],
            *[pltpu.VMEM((n, PROMPT, HEAD_DIM), BF16) for n in (2 * half, trees, trees, 2 * half)],
            dma((5,)), dma((local_kv,)), dma((kv_heads,)), dma((kv_heads,)),
            dma((2,)), dma((2,)), dma((2, heads)), dma((2,)), dma((1,)), dma((1,)),
            dma((kv_heads,)), dma((heads, half)), dma((kv_heads,)), dma((kv_heads,)),
            dma((1,)), dma((1,)), dma((kv_heads,)), dma((4,)),
            dma((4, max(trees, 2 * half))), dma((4, max(trees, 2 * half))),
        ]
        smem = pl.BlockSpec(memory_space=pltpu.SMEM)
        anywhere = pl.BlockSpec(memory_space=pl.ANY)
        grads = pl.pallas_call(
            functools.partial(kernel, heads, trees, kv_heads, group, lengths.shape[1]),
            out_shape=(
                jax.ShapeDtypeStruct(queries.shape, BF16),
                jax.ShapeDtypeStruct(keys.shape, BF16),
                jax.ShapeDtypeStruct(values.shape, BF16),
            ),
            in_specs=[smem] * 4 + [anywhere] * 4,
            out_specs=(anywhere,) * 3,
            scratch_shapes=scratch,
            compiler_params=pltpu.CompilerParams(
                collective_id=0, has_side_effects=True, vmem_limit_bytes=56 * 1024 * 1024
            ),
        )(lengths, guests, advantage, partner, queries, keys, values, upstream)
        return pl.pallas_call(
            hand_over,
            out_shape=tuple(jax.ShapeDtypeStruct(x.shape, x.dtype) for x in grads),
            in_specs=[anywhere] * 3,
            out_specs=(anywhere,) * 3,
            scratch_shapes=[*[pltpu.VMEM(x.shape, x.dtype) for x in grads], dma((2, 12))],
        )(*grads)

    return jax.shard_map(
        step,
        mesh=mesh,
        in_specs=(
            P(("seq", "head"), None),
            P(("seq", "head"), None),
            P(("seq", "head"), None),
            P("seq", "head"),
            P("seq", None),
            P("seq", None),
            P("seq", None),
            P(),
        ),
        out_specs=(P(("seq", "head"), None), P(("seq", "head"), None), P(("seq", "head"), None)),
        check_vma=False,
    )
```

```python
import functools
import math

import jax
import jax.numpy as jnp
from jax import lax
from jax.experimental import pallas as pl
from jax.experimental.pallas import tpu as pltpu
from jax.sharding import PartitionSpec as P

HEAD_DIM = 128
PROMPT = 48
RESP_LEN = 122
TILE = 128
PAD = 128
HALO = 128
LOGICAL = pl.DeviceIdType.MESH
BF16 = jnp.bfloat16
F32 = jnp.float32


def mix(a, b, size):
    out = 0
    bit = 1
    while bit < size:
        out = out + lax.rem(lax.div(a, bit) + lax.div(b, bit), 2) * bit
        bit *= 2
    return out


def dot(a, b, da, db):
    return lax.dot_general(a, b, (((da,), (db,)), ((), ())), preferred_element_type=F32)


def kernel(
    heads, trees, kv_heads, group, resp,
    len_ref, guest_ref, adv_ref, partner_ref,
    q_hbm, k_hbm, v_hbm, up_hbm,
    gq_hbm, gk_hbm, gv_hbm,
    qv, cot, kx, vx, bias, weight, seen_scores, seen_top, gqv, pg, pf, rg, hg, hr, acc, fin, fout, gkv, gvv,
    there, there_mid, there_pick, there_out, far, back, back_mid, back_pick, back_out,
    loc, cloc, csend, crecv, hsend, hrecv, psend, precv, fsend, frecv,
    pgsend, pgrecv, hgsend, hgrecv, finsend, finrecv, oq, okv, there_sems, back_sems,
):
    h = lax.axis_index("head")
    s = lax.axis_index("seq")
    rows = q_hbm.shape[0]
    tiles = rows // TILE
    local_kv = kv_heads // heads
    width = group * HEAD_DIM
    half = kv_heads // 2
    pieces = 2 * half
    stride = trees // pieces
    core = lax.rem(h, 2)
    upper = heads // 2
    sums_here = (h == 0) | (h == upper)
    mate = h + 1 - 2 * core
    need = max((rows * b - PROMPT) % RESP_LEN for b in range(1, heads))
    need = -(-need // 16) * 16
    scaling = HEAD_DIM ** (-0.5)

    def send(src, dst, ssem, rsem, **where):
        return pltpu.make_async_remote_copy(
            src_ref=src, dst_ref=dst, send_sem=ssem, recv_sem=rsem, device_id=where, device_id_type=LOGICAL
        )

    def local(src, dst, sem):
        return pltpu.make_async_copy(src, dst, sem)

    own_copies = [
        local(k_hbm, kx.at[pl.ds(PAD + HALO, rows)], loc.at[0]),
        local(v_hbm, vx.at[pl.ds(PAD + HALO, rows)], loc.at[1]),
        local(q_hbm, qv, loc.at[2]),
    ]
    own_prompt = [
        local(k_hbm.at[pl.ds(0, PROMPT)], kx.at[pl.ds(0, PROMPT)], loc.at[3]),
        local(v_hbm.at[pl.ds(0, PROMPT)], vx.at[pl.ds(0, PROMPT)], loc.at[4]),
    ]
    own_cot = [
        local(
            up_hbm.at[pl.ds(pl.multiple_of(h * rows, TILE), rows), pl.ds(i * width, width)],
            cot.at[h * local_kv + i],
            cloc.at[i],
        )
        for i in range(local_kv)
    ]

    barrier = pltpu.get_barrier_semaphore()
    for m in range(1, heads):
        pl.semaphore_signal(barrier, inc=1, device_id={"head": mix(h, m, heads)}, device_id_type=LOGICAL)

    @pl.loop(1, trees)
    def _(d):
        pl.semaphore_signal(barrier, inc=1, device_id={"seq": lax.rem(s + d, trees)}, device_id_type=LOGICAL)

    @pl.when(h == 0)
    def _():
        for c in own_prompt:
            c.start()

    for c in own_copies + own_cot:
        c.start()
    pl.semaphore_wait(barrier, heads + trees - 2)

    def prompt_copy(a, to):
        src, dst = ((k_hbm, kx), (v_hbm, vx))[a]
        return send(
            src.at[pl.ds(0, PROMPT)], dst.at[pl.ds(0, PROMPT)], psend.at[a, to], precv.at[a], head=to
        )

    def halo_copy(a, to):
        src, dst = ((k_hbm, kx), (v_hbm, vx))[a]
        return send(
            src.at[pl.ds(rows - need, need)], dst.at[pl.ds(PAD + HALO - need, need)], hsend.at[a], hrecv.at[a],
            head=to,
        )

    def cot_copy(m, i):
        p = mix(h, m, heads)
        return send(
            up_hbm.at[pl.ds(pl.multiple_of(p * rows, TILE), rows), pl.ds(i * width, width)],
            cot.at[h * local_kv + i],
            csend.at[m * local_kv + i],
            crecv.at[h * local_kv + i],
            head=p,
        )

    def pass_on(a):
        dst = (kx, vx)[a].at[pl.ds(0, PROMPT)]
        return send(dst, dst, psend.at[a, 0], precv.at[a], head=h + 1)

    first_hop = [1] + list(range(2, heads, 2))

    @pl.when(h == 0)
    def _():
        for to in reversed(first_hop):
            for a in range(2):
                prompt_copy(a, to).start()

    @pl.when(h < heads - 1)
    def _():
        for a in range(2):
            halo_copy(a, h + 1).start()

    n_far = (heads - 2) * local_kv

    def far_chunk(n):
        return cot_copy(2 + lax.div(n, local_kv), lax.rem(n, local_kv))

    for i in range(local_kv):
        cot_copy(1, i).start()
    for n in range(min(2, n_far)):
        far_chunk(jnp.int32(n)).start()

    zero_pad = jnp.zeros((PAD - 2 * PROMPT, kx.shape[1]), BF16)
    kx[pl.ds(2 * PROMPT, PAD - 2 * PROMPT), :] = zero_pad
    vx[pl.ds(2 * PROMPT, PAD - 2 * PROMPT), :] = zero_pad

    if need < HALO:
        zero_rest = jnp.zeros((HALO - need, kx.shape[1]), BF16)
        kx[pl.ds(PAD, HALO - need), :] = zero_rest
        vx[pl.ds(PAD, HALO - need), :] = zero_rest

    @pl.when(h == 0)
    def _():
        zero_halo = jnp.zeros((need, kx.shape[1]), BF16)
        kx[pl.ds(PAD + HALO - need, need), :] = zero_halo
        vx[pl.ds(PAD + HALO - need, need), :] = zero_halo
        for c in own_prompt:
            c.wait()

    @pl.when(h > 0)
    def _():
        for a in range(2):
            prompt_copy(a, h).wait_recv()

    @pl.when((h > 1) & (core == 0))
    def _():
        for a in range(2):
            pass_on(a).start()

    def to_middle(bufs, sems, q):
        out, mid, _, _ = bufs
        return send(out.at[q], mid.at[s], sems.at[0, q], sems.at[1, s], seq=q * stride)

    def from_middle(bufs, sems, d):
        _, _, pick, done = bufs
        q = lax.div(s, stride)
        return send(pick.at[d], done.at[q], sems.at[2, d], sems.at[3, q], seq=d)

    def start_exchange(bufs, sems):
        out, mid, _, _ = bufs
        for q in range(pieces):

            @pl.when(s != q * stride)
            def _():
                to_middle(bufs, sems, q).start()

            @pl.when(s == q * stride)
            def _():
                mid[s] = out[q]

    def turn_exchange(bufs, sems):
        out, mid, pick, done = bufs

        @pl.when(lax.rem(s, stride) == 0)
        def _():
            @pl.loop(1, trees)
            def _(d):
                t = lax.rem(s + d, trees)
                send(out.at[0], mid.at[t], sems.at[0, 0], sems.at[1, t], seq=t).wait_recv()

            @pl.loop(1, trees)
            def _(d):
                t = lax.rem(s + d, trees)
                pick[t] = mid[partner_ref[t]]
                from_middle(bufs, sems, t).start()

            done[lax.div(s, stride)] = mid[partner_ref[s]]

    def finish_exchange(bufs, sems):
        _, _, pick, done = bufs
        for q in range(pieces):

            @pl.when(s != q * stride)
            def _():
                send(pick.at[0], done.at[q], sems.at[2, 0], sems.at[3, q], seq=q * stride).wait_recv()

    def sent_exchange(bufs, sems):
        for q in range(pieces):

            @pl.when(s != q * stride)
            def _():
                to_middle(bufs, sems, q).wait_send()

        @pl.when(lax.rem(s, stride) == 0)
        def _():
            @pl.loop(1, trees)
            def _(d):
                from_middle(bufs, sems, lax.rem(s + d, trees)).wait_send()

    there_bufs = (there, there_mid, there_pick, there_out)
    back_bufs = (back, back_mid, back_pick, back_out)

    def lanes(side, i):
        return pl.ds(pl.multiple_of((side * half + i) * HEAD_DIM, HEAD_DIM), HEAD_DIM)

    for i in range(half):
        there[i] = kx[0:PROMPT, lanes(core, i)]
        there[half + i] = vx[0:PROMPT, lanes(core, i)]
    start_exchange(there_bufs, there_sems)

    row_w = lax.broadcasted_iota(jnp.int32, (rows, HEAD_DIM), 0) + h * rows
    w = jnp.ones((rows, HEAD_DIM), F32)
    for r in range(resp):
        begin = PROMPT + r * RESP_LEN
        inside = (row_w >= begin) & (row_w < begin + RESP_LEN)
        w = jnp.where(inside, jnp.where(row_w - begin < len_ref[0, r], adv_ref[0, r], 0.0), w)
    weight[...] = w
    for t in range(tiles):
        row = lax.broadcasted_iota(jnp.int32, (8, TILE), 1) + (h * rows + t * TILE)
        begin_of = jnp.full((8, TILE), 1 << 20, jnp.int32)
        guest = jnp.zeros((8, TILE), jnp.int32)
        for r in range(resp):
            begin = PROMPT + r * RESP_LEN
            inside = (row >= begin) & (row < begin + RESP_LEN)
            begin_of = jnp.where(inside, begin, begin_of)
            guest = jnp.where(inside, guest_ref[0, r], guest)
        row, begin_of, guest = row[0:1], begin_of[0:1], guest[0:1]
        col = lax.broadcasted_iota(jnp.int32, (PAD, TILE), 0)
        seen_own = (col < PROMPT) & (guest == 0) & (col <= row)
        seen_far = (col >= PROMPT) & (col < 2 * PROMPT) & (guest == 1)
        bias[t, 0:PAD, :] = jnp.where(seen_own | seen_far, 0.0, -1e30)
        key = lax.broadcasted_iota(jnp.int32, (2 * TILE, TILE), 0) + (h * rows + (t - 1) * TILE)
        bias[t, PAD:, :] = jnp.where((key >= begin_of) & (key <= row), 0.0, -1e30)

    for c in own_copies:
        c.wait()

    @pl.when(h > 0)
    def _():
        for a in range(2):
            halo_copy(a, h).wait_recv()

    def stacked(j, t):
        return jnp.concatenate(
            [
                qv[
                    t * TILE : (t + 1) * TILE,
                    pl.ds(pl.multiple_of(j * width + g * HEAD_DIM, HEAD_DIM), HEAD_DIM),
                ]
                for g in range(group)
            ],
            axis=0,
        )

    def score_rows(j):
        cols = pl.ds(pl.multiple_of(j * HEAD_DIM, HEAD_DIM), HEAD_DIM)
        for t in range(tiles):
            win = slice(PAD + t * TILE, PAD + (t + 2) * TILE)
            sc = dot(kx[win, cols], stacked(j, t), 1, 1)
            sc = sc + jnp.concatenate([bias[t, PAD:, :]] * group, axis=1)
            seen_scores[j, t] = sc
            seen_top[j, t] = jnp.max(sc, axis=0, keepdims=True)

    @pl.loop(0, kv_heads // 2)
    def _(j):
        score_rows(j)

    turn_exchange(there_bufs, there_sems)

    @pl.loop(kv_heads // 2, kv_heads)
    def _(j):
        score_rows(j)

    finish_exchange(there_bufs, there_sems)

    def far_copy():
        return send(there_out, far, fsend.at[0], frecv.at[0], head=mate)

    far_copy().start()
    low = slice(PROMPT, 2 * PROMPT)
    for i in range(half):
        kx[low, lanes(core, i)] = there_out[i]
        vx[low, lanes(core, i)] = there_out[half + i]
    far_copy().wait_recv()
    for i in range(half):
        kx[low, lanes(1 - core, i)] = far[i]
        vx[low, lanes(1 - core, i)] = far[half + i]

    def part_copy(j, src, o):
        return send(
            pg.at[j], rg.at[src, lax.rem(j, half)], pgsend.at[j], pgrecv.at[src, lax.rem(j, half)], head=o
        )

    def part_arrival(src, i):
        return send(pg.at[0], rg.at[src, i], pgsend.at[0], pgrecv.at[src, i], head=src)

    def strip_copy(j, to):
        return send(
            hg.at[j, pl.ds(HALO - need, need)], hr.at[j], hgsend.at[j], hgrecv.at[j], head=to
        )

    def out_copy(j):
        return local(gqv.at[j], gq_hbm.at[:, pl.ds(pl.multiple_of(j * width, width), width)], oq.at[j])

    @pl.loop(0, kv_heads)
    def _(n):
        m = lax.div(n, local_kv)
        i = lax.rem(n, local_kv)
        p = mix(h, m, heads)
        j = p * local_kv + i

        @pl.when(m == 0)
        def _():
            local(
                up_hbm.at[pl.ds(0, rows), pl.ds(0, width)], cot.at[j], cloc.at[i]
            ).wait()

        @pl.when(m > 0)
        def _():
            send(cot.at[j], cot.at[j], csend.at[j], crecv.at[j], head=p).wait_recv()

        cols = pl.ds(pl.multiple_of(j * HEAD_DIM, HEAD_DIM), HEAD_DIM)
        k_prompt, v_prompt = kx[0:PAD, cols], vx[0:PAD, cols]
        dk_parts = [None] * (tiles + 2)
        dv_parts = [None] * (tiles + 2)

        def add(parts, at, x):
            parts[at] = x if parts[at] is None else parts[at] + x

        for t in range(tiles):
            span = slice(t * TILE, (t + 1) * TILE)
            win = slice(PAD + t * TILE, PAD + (t + 2) * TILE)
            k_win = jnp.concatenate([k_prompt, kx[win, cols]], axis=0)
            v_win = jnp.concatenate([v_prompt, vx[win, cols]], axis=0)
            q4 = stacked(j, t)
            wt = weight[span, :]
            c4 = jnp.concatenate(
                [
                    (cot[j, span, g * HEAD_DIM : (g + 1) * HEAD_DIM].astype(F32) * wt).astype(BF16)
                    for g in range(group)
                ],
                axis=0,
            )
            first = dot(k_prompt, q4, 1, 1) + jnp.concatenate([bias[t, 0:PAD, :]] * group, axis=1)
            top = jnp.maximum(jnp.max(first, axis=0, keepdims=True), seen_top[j, t])
            sc = jnp.concatenate([first, seen_scores[j, t]], axis=0)
            e = jnp.exp2((sc - top) * (scaling * math.log2(math.e)))
            prob = e * (1.0 / jnp.sum(e, axis=0, keepdims=True))
            gp = dot(v_win, c4, 1, 1)
            inner = jnp.sum(prob * gp, axis=0, keepdims=True)
            ds_low = (prob * (gp - inner)).astype(BF16)
            dv = dot(prob.astype(BF16), c4, 1, 0)
            dk = dot(ds_low, q4, 1, 0)
            dq = (dot(k_win, ds_low, 0, 0) * scaling).astype(BF16).T
            for g in range(group):
                gqv[j, span, g * HEAD_DIM : (g + 1) * HEAD_DIM] = dq[g * TILE : (g + 1) * TILE]
            add(dk_parts, 0, dk[0:PAD])
            add(dv_parts, 0, dv[0:PAD])
            for u in range(2):
                add(dk_parts, 1 + t + u, dk[PAD + u * TILE : PAD + (u + 1) * TILE])
                add(dv_parts, 1 + t + u, dv[PAD + u * TILE : PAD + (u + 1) * TILE])
        out_copy(j).start()
        both = [
            jnp.concatenate([a * scaling, b], axis=1) for a, b in zip(dk_parts, dv_parts)
        ]

        owner = (1 - lax.div(j, half)) * upper

        @pl.when(h == owner)
        def _():
            pf[lax.rem(j, half)] = both[0][0 : 2 * PROMPT]

        @pl.when(h != owner)
        def _():
            pg[j] = both[0][0 : 2 * PROMPT].astype(BF16)
            part_copy(j, h, owner).start()

        @pl.when(h > 0)
        def _():
            hg[j] = both[1].astype(BF16)
            strip_copy(j, h - 1).start()

        for t in range(tiles):
            acc[j, t * TILE : (t + 1) * TILE, :] = both[2 + t]

        @pl.when(n < n_far - 2)
        def _():
            far_chunk(n).wait_send()
            far_chunk(n + 2).start()

    @pl.when(sums_here)
    def _():
        for i in range(half):
            total = pf[i]
            for m in range(1, heads):
                part_arrival(mix(h, m, heads), i).wait_recv()
                total = total + rg[mix(h, m, heads), i].astype(F32)
            pf[i] = total
            back[i] = total[low, 0:HEAD_DIM].astype(BF16)
            back[half + i] = total[low, HEAD_DIM:].astype(BF16)
        start_exchange(back_bufs, back_sems)
        turn_exchange(back_bufs, back_sems)

    @pl.when(h < heads - 1)
    def _():
        for j in range(kv_heads):
            strip_copy(j, h).wait_recv()
            acc[j, rows - need : rows, :] = acc[j, rows - need : rows, :] + hr[j].astype(F32)

    for j in range(kv_heads):
        gkv[:, j * HEAD_DIM : (j + 1) * HEAD_DIM] = acc[j, :, 0:HEAD_DIM].astype(BF16)
        gvv[:, j * HEAD_DIM : (j + 1) * HEAD_DIM] = acc[j, :, HEAD_DIM:].astype(BF16)

    def rows_out(a, begin, count, at):
        src, dst = ((gkv, gk_hbm), (gvv, gv_hbm))[a]
        return local(src.at[pl.ds(begin, count)], dst.at[pl.ds(begin, count)], okv.at[at])

    last = [rows_out(a, PROMPT, rows - PROMPT, a) for a in range(2)]
    top_rows = [rows_out(a, 0, PROMPT, 2 + a) for a in range(2)]
    for c in last:
        c.start()

    def fin_copy():
        return send(fout, fin, finsend.at[0], finrecv.at[0], head=0)

    @pl.when(sums_here)
    def _():
        finish_exchange(back_bufs, back_sems)
        for i in range(half):
            fout[i] = (pf[i, 0:PROMPT, 0:HEAD_DIM] + back_out[i].astype(F32)).astype(BF16)
            fout[half + i] = (pf[i, 0:PROMPT, HEAD_DIM:] + back_out[half + i].astype(F32)).astype(BF16)

    @pl.when(h == upper)
    def _():
        fin_copy().start()

    @pl.when(h == 0)
    def _():
        for o in (1, 0):
            if o == 0:
                send(fout, fin, finsend.at[0], finrecv.at[0], head=upper).wait_recv()
            piece = (fin, fout)[o]
            for i in range(half):
                at = (o * half + i) * HEAD_DIM
                gkv[0:PROMPT, at : at + HEAD_DIM] = piece[i]
                gvv[0:PROMPT, at : at + HEAD_DIM] = piece[half + i]

    for c in top_rows:
        c.start()

    @pl.when(h == 0)
    def _():
        for to in first_hop:
            for a in range(2):
                prompt_copy(a, to).wait_send()

    @pl.when((h > 1) & (core == 0))
    def _():
        for a in range(2):
            pass_on(a).wait_send()

    @pl.when(h < heads - 1)
    def _():
        for a in range(2):
            halo_copy(a, h + 1).wait_send()

    for i in range(local_kv):
        cot_copy(1, i).wait_send()
    for n in range(max(0, n_far - 2), n_far):
        far_chunk(jnp.int32(n)).wait_send()
    far_copy().wait_send()
    sent_exchange(there_bufs, there_sems)
    for j in range(kv_heads):
        o = (1 - j // half) * upper

        @pl.when(h != o)
        def _():
            part_copy(jnp.int32(j), h, o).wait_send()

    @pl.when(sums_here)
    def _():
        sent_exchange(back_bufs, back_sems)

    @pl.when(h > 0)
    def _():
        for j in range(kv_heads):
            strip_copy(j, h - 1).wait_send()

    @pl.when(h == upper)
    def _():
        fin_copy().wait_send()

    for j in range(kv_heads):
        out_copy(j).wait()
    for c in last + top_rows:
        c.wait()


def hand_over(gq, gk, gv, gq_out, gk_out, gv_out, gq_mid, gk_mid, gv_mid, sems):
    ins, outs = [], []
    for src, mid, dst, parts in ((gq, gq_mid, gq_out, 8), (gk, gk_mid, gk_out, 2), (gv, gv_mid, gv_out, 2)):
        size = src.shape[0] // parts
        for i in range(parts):
            at = pl.ds(i * size, size)
            ins.append(pltpu.make_async_copy(src.at[at], mid.at[at], sems.at[0, len(ins)]))
            outs.append(pltpu.make_async_copy(mid.at[at], dst.at[at], sems.at[1, len(outs)]))
    for c in ins:
        c.start()
    for c, d in zip(ins, outs):
        c.wait()
        d.start()
    for d in outs:
        d.wait()


def solution(mesh):
    heads, trees = mesh.shape["head"], mesh.shape["seq"]

    def step(queries, keys, values, upstream, lengths, guests, advantage, partner):
        rows, q_width = queries.shape
        kv_width = keys.shape[1]
        kv_heads = kv_width // HEAD_DIM
        group = q_width // kv_width
        local_kv = kv_heads // heads
        half = kv_heads // 2
        need = max((rows * b - PROMPT) % RESP_LEN for b in range(1, heads))
        need = -(-need // 16) * 16
        width = group * HEAD_DIM
        ext = PAD + HALO + rows
        tiles = rows // TILE
        win = PAD + 2 * TILE
        dma = pltpu.SemaphoreType.DMA
        scratch = [
            pltpu.VMEM((rows, q_width), BF16),
            pltpu.VMEM((kv_heads, rows, width), BF16),
            pltpu.VMEM((ext, kv_width), BF16),
            pltpu.VMEM((ext, kv_width), BF16),
            pltpu.VMEM((tiles, win, TILE), F32),
            pltpu.VMEM((rows, HEAD_DIM), F32),
            pltpu.VMEM((kv_heads, tiles, 2 * TILE, group * TILE), F32),
            pltpu.VMEM((kv_heads, tiles, 1, group * TILE), F32),
            pltpu.VMEM((kv_heads, rows, width), BF16),
            pltpu.VMEM((kv_heads, 2 * PROMPT, 256), BF16),
            pltpu.VMEM((half, 2 * PROMPT, 256), F32),
            pltpu.VMEM((heads, half, 2 * PROMPT, 256), BF16),
            pltpu.VMEM((kv_heads, HALO, 256), BF16),
            pltpu.VMEM((kv_heads, need, 256), BF16),
            pltpu.VMEM((kv_heads, rows, 256), F32),
            pltpu.VMEM((2 * half, PROMPT, HEAD_DIM), BF16),
            pltpu.VMEM((2 * half, PROMPT, HEAD_DIM), BF16),
            pltpu.VMEM((rows, kv_width), BF16),
            pltpu.VMEM((rows, kv_width), BF16),
            *[pltpu.VMEM((n, PROMPT, HEAD_DIM), BF16) for n in (2 * half, trees, trees, 2 * half, 2 * half)],
            *[pltpu.VMEM((n, PROMPT, HEAD_DIM), BF16) for n in (2 * half, trees, trees, 2 * half)],
            dma((5,)), dma((local_kv,)), dma((kv_heads,)), dma((kv_heads,)),
            dma((2,)), dma((2,)), dma((2, heads)), dma((2,)), dma((1,)), dma((1,)),
            dma((kv_heads,)), dma((heads, half)), dma((kv_heads,)), dma((kv_heads,)),
            dma((1,)), dma((1,)), dma((kv_heads,)), dma((4,)),
            dma((4, max(trees, 2 * half))), dma((4, max(trees, 2 * half))),
        ]
        smem = pl.BlockSpec(memory_space=pltpu.SMEM)
        anywhere = pl.BlockSpec(memory_space=pl.ANY)
        grads = pl.pallas_call(
            functools.partial(kernel, heads, trees, kv_heads, group, lengths.shape[1]),
            out_shape=(
                jax.ShapeDtypeStruct(queries.shape, BF16),
                jax.ShapeDtypeStruct(keys.shape, BF16),
                jax.ShapeDtypeStruct(values.shape, BF16),
            ),
            in_specs=[smem] * 4 + [anywhere] * 4,
            out_specs=(anywhere,) * 3,
            scratch_shapes=scratch,
            compiler_params=pltpu.CompilerParams(
                collective_id=0, has_side_effects=True, vmem_limit_bytes=56 * 1024 * 1024
            ),
        )(lengths, guests, advantage, partner, queries, keys, values, upstream)
        return pl.pallas_call(
            hand_over,
            out_shape=tuple(jax.ShapeDtypeStruct(x.shape, x.dtype) for x in grads),
            in_specs=[anywhere] * 3,
            out_specs=(anywhere,) * 3,
            scratch_shapes=[*[pltpu.VMEM(x.shape, x.dtype) for x in grads], dma((2, 12))],
        )(*grads)

    return jax.shard_map(
        step,
        mesh=mesh,
        in_specs=(
            P(("seq", "head"), None),
            P(("seq", "head"), None),
            P(("seq", "head"), None),
            P("seq", "head"),
            P("seq", None),
            P("seq", None),
            P("seq", None),
            P(),
        ),
        out_specs=(P(("seq", "head"), None), P(("seq", "head"), None), P(("seq", "head"), None)),
        check_vma=False,
    )
```
